32 devices in a mesh: groups: 2 (over y), branch: 4 (over x, core), head: 4 (over z).
Axes of the slice: x: 2, y: 2, z: 4, core: 2. Of those that a mesh axis runs over, the one named last changes fastest.
Arguments:
- hidden_in: bfloat16 [256, 8192], P(('groups', 'branch')), parts along dimension 0, may hold values from -40 to 40
- input_gain: bfloat16 [8192], replicated, may hold values from 0.099609375 to 1.8984375
- w_query: bfloat16 [8192, 8192], P('branch', 'head'), may hold values from -0.0625 to 0.0625
- b_query: bfloat16 [8192], P('head'), may hold values from -6 to 6
- w_key: bfloat16 [8192, 1024], P('branch', 'head'), may hold values from -0.0625 to 0.0625
- b_key: bfloat16 [1024], P('head'), may hold values from -6 to 6
- w_value: bfloat16 [8192, 1024], P('branch', 'head'), may hold values from -0.0625 to 0.0625
- b_value: bfloat16 [1024], P('head'), may hold values from -6 to 6
- key_pages: bfloat16 [512, 128, 1024], P(('groups', 'branch'), None, 'head'), parts along dimension 0, may hold values from -1300 to 1300
- value_pages: bfloat16 [512, 128, 1024], P(('groups', 'branch'), None, 'head'), parts along dimension 0, may hold values from -12 to 12
- path_pages: int32 [32], P(('groups', 'branch')), parts along dimension 0, may hold values from 1 to 32, as said below
- page_table: int32 [32, 32], P(('groups', 'branch')), parts along dimension 0, may hold values from 0 to 63, as said below
- parent_index: int32 [256], P(('groups', 'branch')), parts along dimension 0, may hold values from 0 to 15, as said below
- w_out: bfloat16 [8192, 8192], P('head', 'branch'), may hold values from -0.0625 to 0.0625
- post_gain: bfloat16 [8192], replicated, may hold values from 0.099609375 to 1.8984375
- w_gate: bfloat16 [8192, 15360], P('branch', 'head'), may hold values from -0.0625 to 0.0625
- w_up: bfloat16 [8192, 15360], P('branch', 'head'), may hold values from -0.0625 to 0.0625
- w_down: bfloat16 [15360, 8192], P('head', 'branch'), may hold values from -0.046875 to 0.046875
Outputs:
- layer_out: bfloat16 [256, 8192], P(('groups', 'head'), 'branch'), parts along dimension 0
The draws below stay inside these ranges and needn't reach their ends.
There are 2 independent parts, one for each index of `groups`. The reference program is written for one: setup_inputs(seed, part) draws one part's arguments, and reference() takes and returns one part's arrays. A program takes and returns all parts, laid end to end along the dimension named above; an argument that names none is the same for every part. Nothing has to cross between parts.
Inputs may be any that keep to these rules, and one draw needn't show every extreme that they name: `parent_index`: children lie 32 to a device along branch, in row order; the parent of a child lies on device parent // 4. Among the children of one device at most 8 have parents on one device, and some device has exactly 8 such children from every device. `path_pages`: paths are whole pages; the 4 paths of one device take 64 pages or fewer together, and on every device one path has exactly 32 pages. `page_table`: entries j < path_pages[p] of row p are distinct from all other such entries of the parents of the same device; entries past a path's length are to be ignored.
All inputs are finite; a program needn't handle non-finite values.
Results may differ from the reference program's by a relative error of at most 0.025.
Values may be sent and summed in bfloat16 or wider, within the bound.
No kernel may reach another device: no remote copies, remote signals or barrier semaphores. Data moves between devices by JAX's collectives and lax.ppermute only.
A program may use at most 192 MiB of HBM per device.

```python
import math
import jax
import jax.numpy as jnp
from jax import lax

D = 8192
HEADS = 64
KVH = 8
HD = 128
FFW = 15360
PAGE = 128
MAXP = 32
POOL = 64
P_DEV = 4
C_DEV = 32
CAP = 8
PARENTS = 16
CHILDREN = 128
POOLS = 256
QW = 8192
KVW = 1024


def pool_layout(key):
    key_small, key_order, key_slots = jax.random.split(key, 3)
    hosts = PARENTS // P_DEV
    small_top = max(1, (POOL - MAXP) // (P_DEV - 1))
    small = jax.random.randint(key_small, (hosts, P_DEV), 1, small_top + 1, dtype=jnp.int32)
    leading = jnp.arange(P_DEV, dtype=jnp.int32) == 0
    lengths_first = jnp.where(leading[None, :], MAXP, small).astype(jnp.int32)
    order = jax.vmap(lambda sub_key: jax.random.permutation(sub_key, P_DEV))(jax.random.split(key_order, hosts))
    lengths = jnp.take_along_axis(lengths_first, order, 1)
    offsets = jnp.cumsum(lengths, 1) - lengths
    slots = jax.vmap(lambda sub_key: jax.random.permutation(sub_key, POOL))(jax.random.split(key_slots, hosts)).astype(jnp.int32)
    index = (offsets[:, :, None] + jnp.arange(MAXP, dtype=jnp.int32)[None, None, :]) % POOL
    table = jnp.take_along_axis(jnp.broadcast_to(slots[:, None, :], (hosts, P_DEV, POOL)), index, 2)
    return (lengths.reshape(PARENTS).astype(jnp.int32), table.reshape(PARENTS, MAXP).astype(jnp.int32))


def draw_path_pages(key, part):
    lengths, table = pool_layout(key)
    return lengths


def draw_page_table(key, part):
    lengths, table = pool_layout(key)
    return table


def draw_parent_index(key, part):
    key = jax.random.fold_in(key, 13)
    hosts = CHILDREN // C_DEV
    slot_count = hosts * CAP
    key_busy, key_rank, key_rows, key_local = jax.random.split(key, 4)
    busiest = jax.random.randint(key_busy, (), 0, hosts, dtype=jnp.int32)
    ranking = jax.random.permutation(key_rank, hosts).astype(jnp.int32)
    destination = jnp.arange(slot_count, dtype=jnp.int32) // CAP

    def one_host(sub_key):
        key_perm, key_shuffle = jax.random.split(sub_key)
        shuffled = jax.random.permutation(key_perm, slot_count).astype(jnp.int32)
        scores = (shuffled + 4 * ranking[destination]) * slot_count + shuffled
        scores = scores - (destination == busiest).astype(jnp.int32) * (8 * slot_count * slot_count)
        picked = jnp.argsort(scores, stable=True)[:C_DEV]
        picked = picked[jax.random.permutation(key_shuffle, C_DEV)]
        return (picked // CAP).astype(jnp.int32)
    dests = jax.vmap(one_host)(jax.random.split(key_rows, hosts))
    local = jax.random.randint(key_local, (hosts, C_DEV), 0, P_DEV, dtype=jnp.int32)
    return (dests * P_DEV + local).reshape(CHILDREN).astype(jnp.int32)


def draw_hidden_in(key, part):
    key = jax.random.fold_in(key, 11)
    key_base, key_cols, key_rows = jax.random.split(key, 3)
    column = jnp.arange(D, dtype=jnp.float32) / D
    col_scale = jnp.exp(math.log(3.0) * column) * jnp.exp(jax.random.uniform(key_cols, (D,), minval=0.0, maxval=1.2))
    row_scale = jnp.exp(jax.random.uniform(key_rows, (CHILDREN, 1), minval=math.log(0.2), maxval=math.log(2.0)))
    base = jnp.clip(jax.random.normal(key_base, (CHILDREN, D)), -6.0, 6.0)
    return (0.25 * base * col_scale * row_scale).astype(jnp.bfloat16)


def draw_key_pages(key, part):
    key = jax.random.fold_in(key, 12)
    key_base = jax.random.fold_in(key, 0)
    base = jnp.clip(jax.random.normal(key_base, (POOLS, PAGE, KVW)), -6.0, 6.0)
    return base.astype(jnp.bfloat16)


def block_scale(own_key, extent, cuts, low, high):
    factor_of = 1.0
    for axis_at, blocks in cuts:
        heights = jax.random.uniform(jax.random.fold_in(jax.random.fold_in(own_key, 6), axis_at), (blocks,), jnp.float32, low / len(cuts), high / len(cuts))
        factor_of = factor_of * jnp.repeat(jnp.exp(heights), extent[axis_at] // blocks).reshape((-1,) + (1,) * (len(extent) - 1 - axis_at))
    return factor_of


def centred(key, extent, deviation, most, shards=(), kind=jnp.bfloat16):
    array = jax.random.normal(key, extent, jnp.float32) * deviation
    if len(shards) > 0:
        array = block_scale(key, extent, shards, -0.22, 0.18) * array
    return jnp.clip(array, min=-most, max=most).astype(kind)


def setup_inputs(seed: int = 0, part: int = 0) -> dict:
    key_of = jax.random.split(jax.random.key(seed), 19)
    part_keys = jax.random.split(jax.random.fold_in(key_of[18], part), 19)
    hidden_in = draw_hidden_in(jax.random.fold_in(jax.random.fold_in(key_of[18], part), 71), part)
    input_gain = jnp.clip(1.0 + 0.18 * jax.random.normal(key_of[1], (D,), jnp.float32), 0.099609375, 1.8984375).astype(jnp.bfloat16)
    w_query = centred(key_of[2], (D, QW), D ** -0.5, 0.0625, ((0, 4), (1, 4)))
    b_query = centred(key_of[3], (QW,), 1.0, 6.0, ((0, 4),))
    w_key = centred(key_of[4], (D, KVW), D ** -0.5, 0.0625, ((0, 4), (1, 4)))
    b_key = centred(key_of[5], (KVW,), 1.0, 6.0, ((0, 4),))
    w_value = centred(key_of[6], (D, KVW), D ** -0.5, 0.0625, ((0, 4), (1, 4)))
    b_value = centred(key_of[7], (KVW,), 1.0, 6.0, ((0, 4),))
    key_pages = draw_key_pages(jax.random.fold_in(jax.random.fold_in(key_of[18], part), 71), part)
    value_pages = centred(part_keys[9], (POOLS, PAGE, KVW), 2.0, 12.0, ((0, 4), (2, 4)))
    path_pages = draw_path_pages(jax.random.fold_in(jax.random.fold_in(key_of[18], part), 71), part)
    page_table = draw_page_table(jax.random.fold_in(jax.random.fold_in(key_of[18], part), 71), part)
    parent_index = draw_parent_index(jax.random.fold_in(jax.random.fold_in(key_of[18], part), 71), part)
    w_out = centred(key_of[13], (QW, D), QW ** -0.5, 0.0625, ((0, 4), (1, 4)))
    post_gain = jnp.clip(1.0 + 0.18 * jax.random.normal(key_of[14], (D,), jnp.float32), 0.099609375, 1.8984375).astype(jnp.bfloat16)
    w_gate = centred(key_of[15], (D, FFW), D ** -0.5, 0.0625, ((0, 4), (1, 4)))
    w_up = centred(key_of[16], (D, FFW), D ** -0.5, 0.0625, ((0, 4), (1, 4)))
    w_down = centred(key_of[17], (FFW, D), FFW ** -0.5, 0.046875, ((0, 4), (1, 4)))
    return {"hidden_in": hidden_in, "input_gain": input_gain, "w_query": w_query, "b_query": b_query, "w_key": w_key, "b_key": b_key, "w_value": w_value, "b_value": b_value, "key_pages": key_pages, "value_pages": value_pages, "path_pages": path_pages, "page_table": page_table, "parent_index": parent_index, "w_out": w_out, "post_gain": post_gain, "w_gate": w_gate, "w_up": w_up, "w_down": w_down}


EPS = 1e-06
THETA = 1000000.0

def hadamard(order_size):
    index = jnp.arange(order_size, dtype=jnp.int32)
    common = index[:, None] & index[None, :]
    parity = jnp.zeros((order_size, order_size), jnp.int32)
    for bit_level in range(order_size.bit_length() - 1):
        parity = parity ^ common >> bit_level & 1
    return (1 - 2 * parity).astype(jnp.float32) / math.sqrt(order_size)

def rotary(vectors, position):
    width = vectors.shape[-1]
    half_width = width // 2
    freqs = THETA ** (-(jnp.arange(half_width, dtype=jnp.float32) * 2.0 / width))
    angle = position[..., None] * freqs
    first_half = vectors[..., :half_width]
    second_half = vectors[..., half_width:]
    return jnp.concatenate([first_half * jnp.cos(angle) - second_half * jnp.sin(angle), second_half * jnp.cos(angle) + first_half * jnp.sin(angle)], -1)

def reference(hidden_in, input_gain, w_query, b_query, w_key, b_key, w_value, b_value, key_pages, value_pages, path_pages, page_table, parent_index, w_out, post_gain, w_gate, w_up, w_down):
    hidden_f32 = hidden_in.astype(jnp.float32)
    normed = (hidden_f32 * lax.rsqrt(lax.optimization_barrier(jnp.mean(hidden_f32 * hidden_f32, -1, keepdims=True)) + EPS) * input_gain.astype(jnp.float32)).astype(jnp.bfloat16)
    queries = (jnp.dot(normed, w_query, preferred_element_type=jnp.float32) + b_query.astype(jnp.float32)).astype(jnp.bfloat16)
    new_keys = (jnp.dot(normed, w_key, preferred_element_type=jnp.float32) + b_key.astype(jnp.float32)).astype(jnp.bfloat16)
    new_values = (jnp.dot(normed, w_value, preferred_element_type=jnp.float32) + b_value.astype(jnp.float32)).astype(jnp.bfloat16)
    rotation = hadamard(HD)
    group_size = HEADS // KVH
    score_scale = 1.0 / math.sqrt(HD)

    def one_child(inputs):
        query_row, key_row, value_row, parent = inputs
        owner = parent // P_DEV
        pages = (owner * POOL + page_table[parent]).astype(jnp.int32)
        length = path_pages[parent]
        keys_here = jnp.take(key_pages, pages, axis=0).reshape(MAXP * PAGE, KVH, HD)
        values_here = jnp.take(value_pages, pages, axis=0).reshape(MAXP * PAGE, KVH, HD)
        live = jnp.arange(MAXP * PAGE, dtype=jnp.int32) // PAGE < length
        position = length.astype(jnp.float32) * PAGE
        qrope = rotary(query_row.astype(jnp.float32).reshape(HEADS, HD), position)
        krope = rotary(key_row.astype(jnp.float32).reshape(KVH, HD), position)
        vnew = value_row.astype(jnp.float32).reshape(KVH, HD)
        turned = jnp.dot(qrope, rotation, precision=lax.Precision.HIGHEST).astype(jnp.bfloat16)
        turned = lax.optimization_barrier(turned).astype(jnp.float32).reshape(KVH, group_size, HD)
        scores = jnp.einsum('agd,tad->agt', turned, keys_here.astype(jnp.float32)) * score_scale
        own_score = lax.optimization_barrier(jnp.sum(qrope.reshape(KVH, group_size, HD) * krope[:, None, :], -1)) * score_scale
        top = jnp.maximum(lax.optimization_barrier(jnp.max(jnp.where(live, scores, -jnp.inf), -1)), own_score)
        weights = jnp.where(live, jnp.exp(scores - top[..., None]), 0.0)
        own_weight = jnp.exp(own_score - top)
        total = lax.optimization_barrier(jnp.sum(weights, -1)) + own_weight
        weights_b = lax.optimization_barrier(weights.astype(jnp.bfloat16)).astype(jnp.float32)
        mixed = jnp.einsum('agt,tad->agd', weights_b, values_here.astype(jnp.float32))
        unturned = jnp.dot(mixed.reshape(HEADS, HD), rotation, precision=lax.Precision.HIGHEST).reshape(KVH, group_size, HD)
        result = (unturned + own_weight[..., None] * vnew[:, None, :]) / total[..., None]
        return result.astype(jnp.bfloat16).reshape(QW)
    attn = lax.map(one_child, (queries, new_keys, new_values, parent_index))
    mid = hidden_f32 + jnp.dot(attn, w_out, preferred_element_type=jnp.float32)
    normed_ffn = (mid * lax.rsqrt(lax.optimization_barrier(jnp.mean(mid * mid, -1, keepdims=True)) + EPS) * post_gain.astype(jnp.float32)).astype(jnp.bfloat16)
    gate = jnp.dot(normed_ffn, w_gate, preferred_element_type=jnp.float32)
    upward = jnp.dot(normed_ffn, w_up, preferred_element_type=jnp.float32)
    activated = (jax.nn.silu(gate) * upward).astype(jnp.bfloat16)
    layer_out = mid + jnp.dot(activated, w_down, preferred_element_type=jnp.float32)
    return layer_out.astype(jnp.bfloat16)
```

```python
import functools
import math

import jax
import jax.numpy as jnp
import numpy as np
from jax import lax
from jax.experimental import pallas as pl
from jax.experimental.pallas import tpu as pltpu
from jax.sharding import PartitionSpec as P

D = 8192
HD = 128
PAGE = 128
MAXP = 32
POOL = 64
P_DEV = 4
CAP = 8
EXT = 128
CORES = 2

EPS = 1e-06
THETA = 1000000.0
FAR = -1e30
MIB = 1024 * 1024
SPARE = 10 * MIB

F32 = jnp.float32
BF16 = jnp.bfloat16


def hadamard(order_size):
    index = np.arange(order_size)
    common = index[:, None] & index[None, :]
    parity = np.zeros((order_size, order_size), np.int64)
    for bit_level in range(order_size.bit_length() - 1):
        parity = parity ^ (common >> bit_level & 1)
    return ((1 - 2 * parity).astype(np.float32) / np.float32(math.sqrt(order_size))).astype(
        np.float32
    )


SPACES = {"vmem": pltpu.VMEM, "hbm": pltpu.HBM, "any": pl.ANY, "smem": pltpu.SMEM}


def call(kernel, outs, in_spaces, scratch, *args, limit=SPARE, flops=0, moved=0):
    return pl.pallas_call(
        kernel,
        out_shape=[jax.ShapeDtypeStruct(shape, kind) for shape, kind in outs],
        in_specs=[pl.BlockSpec(memory_space=SPACES[space]) for space in in_spaces],
        out_specs=[pl.BlockSpec(memory_space=pltpu.VMEM) for _ in outs],
        scratch_shapes=scratch,
        compiler_params=pltpu.CompilerParams(vmem_limit_bytes=limit),
        cost_estimate=pl.CostEstimate(flops=flops, bytes_accessed=moved, transcendentals=0),
    )(*args)


def fetch_kernel(count, *refs):
    sources, targets, sems = refs[:count], refs[-1 - count : -1], refs[-1]
    copies = [
        pltpu.make_async_copy(source, target, sems.at[at])
        for at, (source, target) in enumerate(zip(sources, targets))
    ]
    for copy in copies:
        copy.start()
    for copy in copies:
        copy.wait()


def fetch(arrays, after, limit=2 * MIB):
    size = sum(array.size * array.dtype.itemsize for array in arrays)
    return pl.pallas_call(
        functools.partial(fetch_kernel, len(arrays)),
        out_shape=[pltpu.VMEM(array.shape, array.dtype) for array in arrays],
        in_specs=[pl.BlockSpec(memory_space=pltpu.HBM)] * len(arrays)
        + [pl.BlockSpec(memory_space=pl.ANY)],
        out_specs=[pl.BlockSpec(memory_space=pltpu.VMEM)] * len(arrays),
        scratch_shapes=[pltpu.SemaphoreType.DMA((len(arrays),))],
        compiler_params=pltpu.CompilerParams(vmem_limit_bytes=limit),
        cost_estimate=pl.CostEstimate(flops=0, bytes_accessed=2 * size, transcendentals=0),
    )(*arrays, after)


def block_width(columns, most):
    best = 128
    for width in range(128, most + 1, 128):
        if columns % width == 0:
            best = width
    return best


class Place:
    def __init__(self, spot, chips, head_count):
        self.chips = chips
        self.head_count = head_count
        self.branch, self.head = spot[0], spot[1]
        self.chip, self.core = self.branch // CORES, self.branch % CORES
        self.steps = [(chip, core) for core in range(CORES) for chip in range(chips)]

    def targets(self):
        return [
            (self.chip + chip) % self.chips * CORES + (self.core + core) % CORES
            for chip, core in self.steps
        ]

    def sources(self):
        return [
            (self.chip + self.chips - chip) % self.chips * CORES + (self.core + core) % CORES
            for chip, core in self.steps
        ]

    def to_heads(self):
        return [(self.head + step) % self.head_count for step in range(self.head_count)]

    def from_heads(self):
        return [
            (self.head + self.head_count - step) % self.head_count
            for step in range(self.head_count)
        ]


def column(devices, length):
    iota = lax.broadcasted_iota(jnp.int32, (length, 1), 0)
    return jnp.concatenate([iota + device * length for device in devices], 0).astype(F32)


def to_row(values):
    size = values.shape[0]
    row_at = lax.broadcasted_iota(jnp.int32, (size, size), 0)
    col_at = lax.broadcasted_iota(jnp.int32, (size, size), 1)
    return jnp.sum(jnp.where(row_at == col_at, values, 0.0), 0, keepdims=True)


def onehot(rows, columns):
    return (rows == to_row(columns)).astype(BF16)


def split_lanes(total):
    rows = total.shape[0]
    high = total.astype(BF16).astype(F32)
    rest = total - high
    middle = rest.astype(BF16).astype(F32)
    low = rest - middle
    lane = lax.broadcasted_iota(jnp.int32, (rows, EXT), 1)
    zero = jnp.zeros((rows, EXT), F32)
    return jnp.where(
        lane == 0, high, jnp.where(lane == 1, middle, jnp.where(lane == 2, low, zero))
    ).astype(BF16)


def dot32(left, right):
    return jnp.dot(left, right, preferred_element_type=F32)


def send_kernel(chips, spot, hidden, parents, *blocks):
    place = Place(spot, chips, 1)
    length, width = hidden.shape[0], blocks[0].shape[1] - EXT
    row_at = lax.broadcasted_iota(jnp.int32, (length, length), 0)
    col_at = lax.broadcasted_iota(jnp.int32, (length, length), 1)
    turned = jnp.sum(
        jnp.where(row_at == col_at, parents[...].astype(F32), 0.0), 1, keepdims=True
    )
    mark = jnp.broadcast_to(turned, (length, EXT)).astype(BF16)
    for ref, device in zip(blocks, place.targets()):
        ref[:, :width] = hidden[:, pl.ds(pl.multiple_of(device * width, width), width)]
        ref[:, width:] = mark


def qkv_kernel(slots, chips, head_count, width, *refs):
    spot = refs[0]
    blocks_n = chips * CORES
    blocks = refs[1 : 1 + blocks_n]
    gain, wq, wk, wv, keep, send, share, codes = refs[1 + blocks_n :]
    place = Place(spot, chips, head_count)
    model_cols = gain.shape[1]
    length = blocks[0].shape[0]
    rows = jnp.concatenate([ref[:, :model_cols] for ref in blocks], 0)
    parent = jnp.concatenate([ref[:, model_cols:] for ref in blocks], 0)[:, :1].astype(F32)
    dest = jnp.floor(parent * (1.0 / P_DEV))
    order = column(place.sources(), length)
    order_row = to_row(order)
    same = (dest == to_row(dest)) & (order_row < order)
    code = dest * slots + jnp.sum(same.astype(F32), 1, keepdims=True)
    lane = lax.broadcasted_iota(jnp.int32, codes.shape, 1)
    codes[...] = jnp.where(lane == 0, code, parent)
    placing = onehot(column(place.targets(), slots), code)
    own = column([place.head], share.shape[0])
    share[...] = dot32((own == order_row).astype(BF16), rows).astype(BF16)
    placed = dot32(placing, rows)
    squares = jnp.sum(placed * placed, 1, keepdims=True)
    scaled = (placed * gain[...]).astype(BF16)
    half = keep.shape[0]
    total_cols = keep.shape[1] - EXT
    keep[:, total_cols:] = jnp.broadcast_to(squares[:half], (half, EXT))
    send[:, total_cols:] = jnp.broadcast_to(squares[half:], (half, EXT))
    at = 0
    for weight in (wq, wk, wv):
        wide = block_width(weight.shape[1], width)
        for step in range(weight.shape[1] // wide):
            product = dot32(scaled, weight[:, step * wide : (step + 1) * wide])
            keep[:, at : at + wide] = product[:half]
            send[:, at : at + wide] = product[half:]
            at += wide


def chip_sum_kernel(slots, keep, got, mine, *others):
    mine[...] = keep[:slots] + got[:slots]
    for at, ref in enumerate(others):
        low, high = (at + 1) * slots, (at + 2) * slots
        total = keep[low:high] + got[low:high]
        ref[:, :-EXT] = total[:, :-EXT].astype(BF16)
        ref[:, -EXT:] = split_lanes(total[:, -EXT:][:, :1])


def attend_kernel(kv_local, group_size, chunk_pages, unroll, received_n, *refs):
    spot, path_pages, mine = refs[:3]
    received = refs[3 : 3 + received_n]
    bq, bk, bv, waves, codes, page_table, turn, kbuf, vbuf = refs[3 + received_n : 12 + received_n]
    out, scores, mixed, sums = refs[12 + received_n :]
    slots = mine.shape[0]
    squares = mine[:, -EXT:][:, :1]
    total = mine[:, :-EXT]
    for ref in received:
        total = total + ref[:, :-EXT].astype(F32)
        squares = squares + jnp.sum(ref[:, -EXT:].astype(F32), 1, keepdims=True)
    bias = jnp.concatenate([ref[...].astype(F32) for ref in (bq, bk, bv)], 1)
    packed = (total * lax.rsqrt(squares * (1.0 / D) + EPS) + bias).astype(BF16).astype(F32)
    heads = kv_local * group_size
    rotation = turn[...]
    code, parent = codes[:, :1], codes[:, 1:2]
    lane = lax.broadcasted_iota(jnp.int32, (1, EXT), 1).astype(F32)
    parent_at = (parent - jnp.floor(parent * (1.0 / P_DEV)) * P_DEV == lane).astype(BF16)
    slot_mark = dot32(onehot(column([spot[0]], slots), code), parent_at)
    wave = jnp.zeros((slots, 2 * HD), F32)
    page_at = lax.broadcasted_iota(jnp.int32, (POOL, MAXP), 0)
    turn_at = lax.broadcasted_iota(jnp.int32, (POOL, MAXP), 1)
    page_mark = jnp.zeros((POOL, EXT), F32)
    for local_parent in range(P_DEV):
        wave = wave + slot_mark[:, local_parent : local_parent + 1] * waves[
            local_parent : local_parent + 1, :
        ]
        live = (page_table[local_parent : local_parent + 1, :] == page_at) & (
            turn_at < path_pages[local_parent]
        )
        owned = jnp.max(live.astype(F32), 1, keepdims=True)
        page_mark = jnp.where(lane == local_parent, (1.0 - owned) * FAR, page_mark)
    page_marks = page_mark.astype(BF16).astype(F32)

    def stacked(first, count):
        return jnp.concatenate(
            [packed[:, (first + at) * HD : (first + at + 1) * HD] for at in range(count)], 0
        )

    def rope(vectors, count):
        cos = jnp.concatenate([wave[:, :HD]] * count, 0)
        sin = jnp.concatenate([wave[:, HD:]] * count, 0)
        return vectors * cos + pltpu.roll(vectors, HD // 2, 1) * sin

    queries = rope(stacked(0, heads), heads)
    new_keys = rope(stacked(heads, kv_local), kv_local)
    turned = jnp.dot(
        queries, rotation, precision=lax.Precision.HIGHEST, preferred_element_type=F32
    ).astype(BF16)
    scale = 1.0 / math.sqrt(HD)
    rate = scale * math.log2(math.e)
    rows = group_size * slots
    chunk = chunk_pages * PAGE
    chunks = POOL // chunk_pages
    marks = jnp.concatenate([slot_mark.astype(BF16)] * group_size, 0)
    sums[:POOL, :] = page_marks
    for kv_at in range(kv_local):
        query_now = queries[kv_at * rows : (kv_at + 1) * rows]
        left = jnp.concatenate([turned[kv_at * rows : (kv_at + 1) * rows], marks], 1)
        key_now = jnp.concatenate([new_keys[kv_at * slots : (kv_at + 1) * slots]] * group_size, 0)
        own_score = jnp.sum(query_now * key_now, 1, keepdims=True)
        span = slice(kv_at * HD, (kv_at + 1) * HD)
        if kv_at > 0:
            sums[:POOL, :] = page_marks

        def first_pass(at, best):
            pages = pl.ds(pl.multiple_of(at * chunk_pages, chunk_pages), chunk_pages)
            page_keys = kbuf[pages, :, span].reshape(chunk, HD)
            mark = jnp.broadcast_to(
                sums[pages, :][:, None, :], (chunk_pages, PAGE, EXT)
            ).reshape(chunk, EXT)
            now = lax.dot_general(
                left,
                jnp.concatenate([page_keys, mark.astype(BF16)], 1),
                (((1,), (1,)), ((), ())),
                preferred_element_type=F32,
            )
            scores[at] = now
            for page in range(chunk_pages):
                best = jnp.maximum(best, now[:, page * PAGE : (page + 1) * PAGE])
            return best

        best = lax.fori_loop(
            0, chunks, first_pass, jnp.full((rows, PAGE), -jnp.inf, F32), unroll=unroll
        )
        top = jnp.maximum(jnp.max(best, 1, keepdims=True), own_score)
        top_rate = top * rate
        sums[...] = jnp.zeros_like(sums)
        mixed[...] = jnp.zeros_like(mixed)

        def second_pass(at, carry):
            pages = pl.ds(pl.multiple_of(at * chunk_pages, chunk_pages), chunk_pages)
            weights = jnp.exp2(scores[at] * rate - top_rate)
            part = weights[:, :PAGE]
            for page in range(1, chunk_pages):
                part = part + weights[:, page * PAGE : (page + 1) * PAGE]
            sums[:rows, :] += part
            page_values = vbuf[pages, :, span].reshape(chunk, HD)
            mixed[...] += dot32(weights.astype(BF16), page_values)
            return carry

        lax.fori_loop(0, chunks, second_pass, 0, unroll=unroll)
        own = jnp.exp2(own_score * rate - top_rate)
        whole = jnp.sum(sums[:rows, :], 1, keepdims=True) + own
        unturned = jnp.dot(
            mixed[...], rotation, precision=lax.Precision.HIGHEST, preferred_element_type=F32
        )
        value_at = (heads + kv_local + kv_at) * HD
        value_now = jnp.concatenate([packed[:, value_at : value_at + HD]] * group_size, 0)
        result = ((unturned + own * value_now) / whole).astype(BF16)
        for head in range(group_size):
            at = (kv_at * group_size + head) * HD
            out[:, at : at + HD] = result[head * slots : (head + 1) * slots]


def spread_rows(rows, order, weight, width, mine, others):
    ordered = dot32(order, rows).astype(BF16)
    share = mine.shape[0]
    for step in range(weight.shape[1] // width):
        span = slice(step * width, (step + 1) * width)
        product = dot32(ordered, weight[:, span])
        mine[:, span] = product[:share]
        for at, ref in enumerate(others):
            ref[:, span] = product[(at + 1) * share : (at + 2) * share].astype(BF16)


def mixer_kernel(slots, local_rows, chips, head_count, width, *refs):
    blocks_n = chips * CORES
    spot, codes = refs[:2]
    blocks = refs[2 : 2 + blocks_n]
    weight, mine = refs[2 + blocks_n : 4 + blocks_n]
    place = Place(spot, chips, head_count)
    sources = place.sources()
    slot_rows = onehot(codes[:, :1], column(sources, slots))
    child_rows = onehot(column(place.to_heads(), mine.shape[0]), column(sources, local_rows))
    order = dot32(child_rows, slot_rows).astype(BF16)
    rows = jnp.concatenate([ref[...] for ref in blocks], 0)
    spread_rows(rows, order, weight, width, mine, refs[4 + blocks_n :])


def lower_kernel(first, last, local_rows, chips, head_count, width, *refs):
    blocks_n = chips * CORES
    spot = refs[0]
    blocks = refs[1 : 1 + blocks_n]
    weight = refs[1 + blocks_n]
    before = None if first == 0 else refs[2 + blocks_n]
    outs = refs[(2 if first == 0 else 3) + blocks_n :]
    place = Place(spot, chips, head_count)
    share_rows = chips * CORES * local_rows // head_count
    order = onehot(column(place.to_heads(), share_rows), column(place.sources(), local_rows))
    rows = jnp.concatenate([ref[...] for ref in blocks], 0)
    ordered = dot32(order, rows).astype(BF16)
    deep = rows.shape[1]
    for step in range(weight.shape[1] // width):
        span = slice(step * width, (step + 1) * width)
        product = dot32(ordered, weight[first : first + deep, span])
        if before is not None:
            product = product + before[:, span]
        if not last:
            outs[0][:, span] = product
            continue
        outs[0][:, span] = product[:share_rows]
        for at, ref in enumerate(outs[1:]):
            ref[:, span] = product[(at + 1) * share_rows : (at + 2) * share_rows].astype(BF16)


def residual_kernel(share, mine, gain, *refs):
    received = refs[:-2]
    residual, scaled = refs[-2:]
    total = mine[...]
    for ref in received:
        total = total + ref[...].astype(F32)
    total = share[...].astype(F32) + total
    residual[...] = total
    scaled[:, :-EXT] = (total * gain[...]).astype(BF16)
    scaled[:, -EXT:] = split_lanes(jnp.sum(total * total, 1, keepdims=True))


def gate_columns(ordered, weights, first, count, width, keep, send):
    half = keep.shape[0]
    scaled = ordered[:, :-EXT]
    at = 0
    for weight in weights:
        for step in range(count // width):
            low = first + step * width
            product = dot32(scaled, weight[:, low : low + width])
            keep[:, at : at + width] = product[:half]
            send[:, at : at + width] = product[half:].astype(BF16)
            at += width


def first_gate_kernel(local_rows, chips, head_count, count, width, *refs):
    spot = refs[0]
    blocks = refs[1 : 1 + head_count]
    w_gate, w_up, keep, send, rest = refs[1 + head_count :]
    place = Place(spot, chips, head_count)
    order = onehot(
        column(place.targets(), local_rows), column(place.from_heads(), blocks[0].shape[0])
    )
    rows = jnp.concatenate([ref[...] for ref in blocks], 0)
    ordered = dot32(order, rows).astype(BF16)
    rest[...] = ordered
    half = keep.shape[0]
    keep[:, -EXT:] = ordered[:half, -EXT:].astype(F32)
    send[:, -EXT:] = ordered[half:, -EXT:]
    gate_columns(ordered, (w_gate, w_up), 0, count, width, keep, send)


def next_gate_kernel(first, count, width, ordered, w_gate, w_up, keep, send):
    gate_columns(ordered[...], (w_gate, w_up), first, count, width, keep, send)


def chip_gate_kernel(local_rows, columns, keep, got, mine, *others):
    mine[...] = keep[:local_rows] + got[:local_rows].astype(F32)
    for at, ref in enumerate(others):
        low, high = (at + 1) * local_rows, (at + 2) * local_rows
        total = keep[low:high] + got[low:high].astype(F32)
        ref[:, :columns] = total[:, :columns].astype(BF16)
        if total.shape[1] > columns:
            ref[:, columns:] = split_lanes(jnp.sum(total[:, columns:], 1, keepdims=True))


def gated(mine, received, columns, scale):
    gate = mine[:, :columns]
    up = mine[:, columns : 2 * columns]
    for ref in received:
        gate = gate + ref[:, :columns].astype(F32)
        up = up + ref[:, columns : 2 * columns].astype(F32)
    gate = gate * scale
    up = up * scale
    return (gate / (1.0 + jnp.exp(-gate)) * up).astype(BF16)


def first_activate_kernel(mine, *refs):
    received, _, out, scale_out = refs[:-3], refs[-3], refs[-2], refs[-1]
    squares = jnp.sum(mine[:, -EXT:], 1, keepdims=True)
    for ref in received:
        squares = squares + jnp.sum(ref[:, -EXT:].astype(F32), 1, keepdims=True)
    scale = lax.rsqrt(squares * (1.0 / D) + EPS)
    scale_out[...] = jnp.broadcast_to(scale, scale_out.shape)
    out[...] = gated(mine, received, out.shape[1], scale)


def next_activate_kernel(scale, mine, *refs):
    out = refs[-1]
    out[...] = gated(mine, refs[:-1], out.shape[1], scale[:, :1])


def final_kernel(residual, mine, *refs):
    received, out = refs[:-1], refs[-1]
    total = mine[...]
    for ref in received:
        total = total + ref[...].astype(F32)
    out[...] = (residual[...] + total).astype(BF16)


def local(
    hidden_in,
    input_gain,
    w_query,
    b_query,
    w_key,
    b_key,
    w_value,
    b_value,
    key_pages,
    value_pages,
    path_pages,
    page_table,
    parent_index,
    w_out,
    post_gain,
    w_gate,
    w_up,
    w_down,
):
    branch_count = lax.axis_size("branch")
    head_count = lax.axis_size("head")
    branch_pos = lax.axis_index("branch")
    head_pos = lax.axis_index("head")
    chips = branch_count // CORES
    local_rows = hidden_in.shape[0]
    all_rows = local_rows * branch_count
    share_rows = all_rows // head_count
    model_cols = w_query.shape[0]
    query_cols = w_query.shape[1]
    kv_cols = w_key.shape[1]
    kv_local = kv_cols // HD
    heads_local = query_cols // HD
    group_size = heads_local // kv_local
    slots = branch_count * CAP
    ff_local = w_gate.shape[1]
    packed_cols = query_cols + 2 * kv_cols
    spot = jnp.stack([branch_pos, head_pos]).astype(jnp.int32)
    steps = [(chip, core) for core in range(CORES) for chip in range(chips)]

    def over_branch(array, chip_step, core_step):
        pairs = []
        for source in range(branch_count):
            chip, core = source // CORES, source % CORES
            to = (chip + chip_step) % chips * CORES + (core + core_step) % CORES
            pairs.append((source, to))
        return lax.ppermute(array, "branch", pairs)

    def over_head(array, step):
        pairs = [(source, (source + step) % head_count) for source in range(head_count)]
        return lax.ppermute(array, "head", pairs)

    def gain_slice(gain):
        return lax.dynamic_slice_in_dim(gain, branch_pos * model_cols, model_cols, 0).astype(F32)[
            None
        ]

    outgoing = call(
        functools.partial(send_kernel, chips),
        [((local_rows, model_cols + EXT), BF16)] * branch_count,
        ["smem", "vmem", "vmem"],
        [],
        spot,
        hidden_in,
        parent_index[None],
    )
    hidden_blocks = [outgoing[0]]
    for block, (chip, core) in zip(outgoing[1:], steps[1:]):
        hidden_blocks.append(over_branch(block, chip, core))
    wq, wk, wv = fetch([w_query, w_key, w_value], outgoing[0], 44 * MIB)
    keep, send, share, codes = call(
        functools.partial(qkv_kernel, slots, chips, head_count, 512),
        [
            ((chips * slots, packed_cols + EXT), F32),
            ((chips * slots, packed_cols + EXT), F32),
            ((share_rows, model_cols), BF16),
            ((all_rows, EXT), F32),
        ],
        ["smem"] + ["vmem"] * (branch_count + 4),
        [],
        spot,
        *hidden_blocks,
        gain_slice(input_gain),
        wq,
        wk,
        wv,
        flops=2 * all_rows * model_cols * packed_cols,
    )
    got = over_branch(send, 0, 1)
    mine, *others = call(
        functools.partial(chip_sum_kernel, slots),
        [((slots, packed_cols + EXT), F32)]
        + [((slots, packed_cols + EXT), BF16)] * (chips - 1),
        ["vmem"] * 2,
        [],
        keep,
        got,
    )
    received = [over_branch(other, at + 1, 0) for at, other in enumerate(others)]
    keys, values = fetch([key_pages, value_pages], others[0])

    freqs = THETA ** (-(jnp.arange(HD // 2, dtype=F32) * 2.0 / HD))
    angle = (path_pages.astype(F32) * PAGE)[:, None] * freqs
    cosine, sine = jnp.cos(angle), jnp.sin(angle)
    waves = jnp.concatenate([cosine, cosine, -sine, sine], 1)
    chunk_pages, unroll = 8, 4
    rows = group_size * slots
    if rows > 512:
        unroll = 1
    score_bytes = 4 * rows * POOL * PAGE
    (attention,) = call(
        functools.partial(attend_kernel, kv_local, group_size, chunk_pages, unroll, chips - 1),
        [((slots, query_cols), BF16)],
        ["smem"] * 2 + ["vmem"] * (chips + 9),
        [
            pltpu.VMEM((POOL // chunk_pages, rows, chunk_pages * PAGE), F32),
            pltpu.VMEM((rows, HD), F32),
            pltpu.VMEM((max(rows, POOL), HD), F32),
        ],
        spot,
        path_pages,
        mine,
        *received,
        b_query[None],
        b_key[None],
        b_value[None],
        waves,
        codes,
        page_table,
        jnp.asarray(hadamard(HD)),
        keys,
        values,
        limit=score_bytes + SPARE + SPARE // 2,
        flops=4 * kv_cols * rows * POOL * PAGE,
    )

    def gather_branch(array):
        near = [array] + [over_branch(array, chip, 0) for chip in range(1, chips)]
        return near + [over_branch(block, 0, 1) for block in near]

    gathered = gather_branch(attention)
    (w_out_near,) = fetch([w_out], attention)
    out_width = block_width(model_cols, 512)
    mixer, *others = call(
        functools.partial(mixer_kernel, slots, local_rows, chips, head_count, out_width),
        [((share_rows, model_cols), F32)] + [((share_rows, model_cols), BF16)] * (head_count - 1),
        ["smem"] + ["vmem"] * (branch_count + 2),
        [],
        spot,
        codes,
        *gathered,
        w_out_near,
        flops=2 * all_rows * w_out.size,
    )
    received = [over_head(other, at + 1) for at, other in enumerate(others)]
    (w_gate_near,) = fetch([w_gate], mixer)
    residual, scaled = call(
        residual_kernel,
        [((share_rows, model_cols), F32), ((share_rows, model_cols + EXT), BF16)],
        ["vmem"] * (head_count + 2),
        [],
        share,
        mixer,
        gain_slice(post_gain),
        *received,
    )
    scaled_blocks = [scaled] + [over_head(scaled, step) for step in range(1, head_count)]
    (w_up_near,) = fetch([w_up], scaled)
    tiles = ff_local // 128
    cuts = [0, (tiles + 1) // 2 * 128, ff_local]
    counts = [high - low for low, high in zip(cuts, cuts[1:])]

    def gate_outs(extra):
        return [((chips * local_rows, extra), F32), ((chips * local_rows, extra), BF16)]

    keep, send, ordered = call(
        functools.partial(
            first_gate_kernel,
            local_rows,
            chips,
            head_count,
            counts[0],
            block_width(counts[0], 768),
        ),
        gate_outs(2 * counts[0] + EXT) + [((all_rows, model_cols + EXT), BF16)],
        ["smem"] + ["vmem"] * (head_count + 2),
        [],
        spot,
        *scaled_blocks,
        w_gate_near,
        w_up_near,
        flops=4 * all_rows * model_cols * counts[0],
    )
    parts = [(keep, over_branch(send, 0, 1))]
    keep, send = call(
        functools.partial(next_gate_kernel, cuts[1], counts[1], block_width(counts[1], 768)),
        gate_outs(2 * counts[1]),
        ["vmem"] * 3,
        [],
        ordered,
        w_gate_near,
        w_up_near,
        flops=4 * all_rows * model_cols * counts[1],
    )
    parts.append((keep, over_branch(send, 0, 1)))
    sums = []
    for (keep, got), count in zip(parts, counts):
        wide = keep.shape[1]
        mine, *others = call(
            functools.partial(chip_gate_kernel, local_rows, 2 * count),
            [((local_rows, wide), F32)] + [((local_rows, wide), BF16)] * (chips - 1),
            ["vmem"] * 2,
            [],
            keep,
            got,
        )
        sums.append((mine, [over_branch(other, at + 1, 0) for at, other in enumerate(others)], others))
    (w_down_near,) = fetch([w_down], sums[1][2][0], 32 * MIB)
    activated, scale = call(
        first_activate_kernel,
        [((local_rows, counts[0]), BF16), ((local_rows, EXT), F32)],
        ["vmem"] * chips + ["any"],
        [],
        sums[0][0],
        *sums[0][1],
        w_down_near,
    )
    gathered = gather_branch(activated)
    (activated,) = call(
        next_activate_kernel,
        [((local_rows, counts[1]), BF16)],
        ["vmem"] * (chips + 1),
        [],
        scale,
        sums[1][0],
        *sums[1][1],
    )
    gathered_next = gather_branch(activated)
    (partial,) = call(
        functools.partial(lower_kernel, 0, False, local_rows, chips, head_count, out_width),
        [((all_rows, model_cols), F32)],
        ["smem"] + ["vmem"] * (branch_count + 1),
        [],
        spot,
        *gathered,
        w_down_near,
        flops=2 * all_rows * model_cols * counts[0],
    )
    lowered, *others = call(
        functools.partial(lower_kernel, cuts[1], True, local_rows, chips, head_count, out_width),
        [((share_rows, model_cols), F32)] + [((share_rows, model_cols), BF16)] * (head_count - 1),
        ["smem"] + ["vmem"] * (branch_count + 2),
        [],
        spot,
        *gathered_next,
        w_down_near,
        partial,
        flops=2 * all_rows * model_cols * counts[1],
    )
    received = [over_head(other, at + 1) for at, other in enumerate(others)]
    (final,) = call(
        final_kernel,
        [((share_rows, model_cols), BF16)],
        ["vmem"] * (head_count + 1),
        [],
        residual,
        lowered,
        *received,
    )
    return final


def solution(mesh):
    placed = (
        P(("groups", "branch"), None),
        P(),
        P("branch", "head"),
        P("head"),
        P("branch", "head"),
        P("head"),
        P("branch", "head"),
        P("head"),
        P(("groups", "branch"), None, "head"),
        P(("groups", "branch"), None, "head"),
        P(("groups", "branch")),
        P(("groups", "branch"), None),
        P(("groups", "branch")),
        P("head", "branch"),
        P(),
        P("branch", "head"),
        P("branch", "head"),
        P("head", "branch"),
    )
    return jax.shard_map(
        local,
        mesh=mesh,
        in_specs=placed,
        out_specs=P(("groups", "head"), "branch"),
        check_vma=False,
    )
```

```python
import functools
import math

import jax
import jax.numpy as jnp
import numpy as np
from jax import lax
from jax.experimental import pallas as pl
from jax.experimental.pallas import tpu as pltpu
from jax.sharding import PartitionSpec as P

D = 8192
HD = 128
PAGE = 128
MAXP = 32
POOL = 64
P_DEV = 4
CAP = 8
EXT = 128
CORES = 2

EPS = 1e-06
THETA = 1000000.0
FAR = -1e30
MIB = 1024 * 1024
SPARE = 10 * MIB
SEND_LIMIT = 63 * MIB

F32 = jnp.float32
BF16 = jnp.bfloat16


def hadamard(order_size):
    index = np.arange(order_size)
    common = index[:, None] & index[None, :]
    parity = np.zeros((order_size, order_size), np.int64)
    for bit_level in range(order_size.bit_length() - 1):
        parity = parity ^ (common >> bit_level & 1)
    return ((1 - 2 * parity).astype(np.float32) / np.float32(math.sqrt(order_size))).astype(
        np.float32
    )


SPACES = {"vmem": pltpu.VMEM, "hbm": pltpu.HBM, "any": pl.ANY, "smem": pltpu.SMEM}


def call(kernel, outs, in_spaces, scratch, *args, limit=SPARE, flops=0, moved=0, near=False):
    return pl.pallas_call(
        kernel,
        out_shape=[
            pltpu.VMEM(shape, kind) if near else jax.ShapeDtypeStruct(shape, kind)
            for shape, kind in outs
        ],
        in_specs=[pl.BlockSpec(memory_space=SPACES[space]) for space in in_spaces],
        out_specs=[pl.BlockSpec(memory_space=pltpu.VMEM) for _ in outs],
        scratch_shapes=scratch,
        compiler_params=pltpu.CompilerParams(vmem_limit_bytes=limit),
        cost_estimate=pl.CostEstimate(flops=flops, bytes_accessed=moved, transcendentals=0),
    )(*args)


def fetch_kernel(count, *refs):
    sources, targets, sems = refs[:count], refs[-1 - count : -1], refs[-1]
    copies = [
        pltpu.make_async_copy(source, target, sems.at[at])
        for at, (source, target) in enumerate(zip(sources, targets))
    ]
    for copy in copies:
        copy.start()
    for copy in copies:
        copy.wait()


def fetch(arrays, after, limit=2 * MIB):
    size = sum(array.size * array.dtype.itemsize for array in arrays)
    return pl.pallas_call(
        functools.partial(fetch_kernel, len(arrays)),
        out_shape=[pltpu.VMEM(array.shape, array.dtype) for array in arrays],
        in_specs=[pl.BlockSpec(memory_space=pltpu.HBM)] * len(arrays)
        + [pl.BlockSpec(memory_space=pl.ANY)],
        out_specs=[pl.BlockSpec(memory_space=pltpu.VMEM)] * len(arrays),
        scratch_shapes=[pltpu.SemaphoreType.DMA((len(arrays),))],
        compiler_params=pltpu.CompilerParams(vmem_limit_bytes=limit),
        cost_estimate=pl.CostEstimate(flops=0, bytes_accessed=2 * size, transcendentals=0),
    )(*arrays, after)


def block_width(columns, most):
    best = 128
    for width in range(128, most + 1, 128):
        if columns % width == 0:
            best = width
    return best


class Place:
    def __init__(self, spot, chips, head_count):
        self.chips = chips
        self.head_count = head_count
        self.branch, self.head = spot[0], spot[1]
        self.chip, self.core = self.branch // CORES, self.branch % CORES
        self.steps = [(chip, core) for core in range(CORES) for chip in range(chips)]

    def targets(self):
        return [
            (self.chip + chip) % self.chips * CORES + (self.core + core) % CORES
            for chip, core in self.steps
        ]

    def sources(self):
        return [
            (self.chip + self.chips - chip) % self.chips * CORES + (self.core + core) % CORES
            for chip, core in self.steps
        ]

    def to_heads(self):
        return [(self.head + step) % self.head_count for step in range(self.head_count)]

    def from_heads(self):
        return [
            (self.head + self.head_count - step) % self.head_count
            for step in range(self.head_count)
        ]


def column(devices, length):
    iota = lax.broadcasted_iota(jnp.int32, (length, 1), 0)
    return jnp.concatenate([iota + device * length for device in devices], 0).astype(F32)


def to_row(values):
    size = values.shape[0]
    row_at = lax.broadcasted_iota(jnp.int32, (size, size), 0)
    col_at = lax.broadcasted_iota(jnp.int32, (size, size), 1)
    return jnp.sum(jnp.where(row_at == col_at, values, 0.0), 0, keepdims=True)


def onehot(rows, columns):
    return (rows == to_row(columns)).astype(BF16)


def split_lanes(total):
    rows = total.shape[0]
    high = total.astype(BF16).astype(F32)
    rest = total - high
    middle = rest.astype(BF16).astype(F32)
    low = rest - middle
    lane = lax.broadcasted_iota(jnp.int32, (rows, EXT), 1)
    zero = jnp.zeros((rows, EXT), F32)
    return jnp.where(
        lane == 0, high, jnp.where(lane == 1, middle, jnp.where(lane == 2, low, zero))
    ).astype(BF16)


def dot32(left, right):
    return jnp.dot(left, right, preferred_element_type=F32)


def send_kernel(chips, hidden, parents, *refs):
    blocks, (listed, sems) = refs[:-2], refs[-2:]
    place = Place((lax.axis_index("branch"), 0), chips, 1)
    length, width = hidden.shape[0], blocks[0].shape[1] - EXT
    copies = [pltpu.make_async_copy(parents, listed, sems.at[0])]
    for at, (ref, device) in enumerate(zip(blocks, place.targets())):
        source = hidden.at[:, pl.ds(pl.multiple_of(device * width, width), width)]
        copies.append(pltpu.make_async_copy(source, ref.at[:, :width], sems.at[at + 1]))
    for copy in copies:
        copy.start()
    copies[0].wait()
    row_at = lax.broadcasted_iota(jnp.int32, (length, length), 0)
    col_at = lax.broadcasted_iota(jnp.int32, (length, length), 1)
    turned = jnp.sum(jnp.where(row_at == col_at, listed[...].astype(F32), 0.0), 1, keepdims=True)
    mark = jnp.broadcast_to(turned, (length, EXT)).astype(BF16)
    for ref in blocks:
        ref[:, width:] = mark
    for copy in copies[1:]:
        copy.wait()


def qkv_kernel(slots, chips, head_count, width, *refs):
    spot = refs[0]
    blocks_n = chips * CORES
    blocks = refs[1 : 1 + blocks_n]
    gain, wq, wk, wv, keep, send, share, codes = refs[1 + blocks_n :]
    place = Place(spot, chips, head_count)
    model_cols = gain.shape[1]
    length = blocks[0].shape[0]
    rows = jnp.concatenate([ref[:, :model_cols] for ref in blocks], 0)
    parent = jnp.concatenate([ref[:, model_cols:] for ref in blocks], 0)[:, :1].astype(F32)
    dest = jnp.floor(parent * (1.0 / P_DEV))
    order = column(place.sources(), length)
    order_row = to_row(order)
    same = (dest == to_row(dest)) & (order_row < order)
    code = dest * slots + jnp.sum(same.astype(F32), 1, keepdims=True)
    lane = lax.broadcasted_iota(jnp.int32, codes.shape, 1)
    codes[...] = jnp.where(lane == 0, code, parent)
    placing = onehot(column(place.targets(), slots), code)
    own = column([place.head], share.shape[0])
    share[...] = dot32((own == order_row).astype(BF16), rows).astype(BF16)
    placed = dot32(placing, rows)
    squares = jnp.sum(placed * placed, 1, keepdims=True)
    scaled = (placed * gain[...]).astype(BF16)
    half = keep.shape[0]
    total_cols = keep.shape[1] - EXT
    keep[:, total_cols:] = jnp.broadcast_to(squares[:half], (half, EXT))
    send[:, total_cols:] = jnp.broadcast_to(squares[half:], (half, EXT))
    at = 0
    for weight in (wq, wk, wv):
        wide = block_width(weight.shape[1], width)
        for step in range(weight.shape[1] // wide):
            product = dot32(scaled, weight[:, step * wide : (step + 1) * wide])
            keep[:, at : at + wide] = product[:half]
            send[:, at : at + wide] = product[half:]
            at += wide


def chip_sum_kernel(slots, keep, got, mine, *others):
    mine[...] = keep[:slots] + got[:slots]
    for at, ref in enumerate(others):
        low, high = (at + 1) * slots, (at + 2) * slots
        total = keep[low:high] + got[low:high]
        ref[:, :-EXT] = total[:, :-EXT].astype(BF16)
        ref[:, -EXT:] = split_lanes(total[:, -EXT:][:, :1])


def attend_kernel(kv_local, group_size, chunk_pages, unroll, received_n, *refs):
    spot, path_pages, mine = refs[:3]
    received = refs[3 : 3 + received_n]
    bq, bk, bv, waves, codes, page_table, turn, kbuf, vbuf = refs[3 + received_n : 12 + received_n]
    out, scores, mixed, page_marks = refs[12 + received_n :]
    slots = mine.shape[0]
    squares = mine[:, -EXT:][:, :1]
    total = mine[:, :-EXT]
    for ref in received:
        total = total + ref[:, :-EXT].astype(F32)
        squares = squares + jnp.sum(ref[:, -EXT:].astype(F32), 1, keepdims=True)
    bias = jnp.concatenate([ref[...].astype(F32) for ref in (bq, bk, bv)], 1)
    packed = (total * lax.rsqrt(squares * (1.0 / D) + EPS) + bias).astype(BF16).astype(F32)
    heads = kv_local * group_size
    rotation = turn[...]
    code, parent = codes[:, :1], codes[:, 1:2]
    lane = lax.broadcasted_iota(jnp.int32, (1, EXT), 1).astype(F32)
    parent_at = (parent - jnp.floor(parent * (1.0 / P_DEV)) * P_DEV == lane).astype(BF16)
    slot_mark = dot32(onehot(column([spot[0]], slots), code), parent_at)
    wave = jnp.zeros((slots, 2 * HD), F32)
    page_at = lax.broadcasted_iota(jnp.int32, (POOL, MAXP), 0)
    turn_at = lax.broadcasted_iota(jnp.int32, (POOL, MAXP), 1)
    page_mark = jnp.zeros((POOL, EXT), F32)
    for local_parent in range(P_DEV):
        wave = wave + slot_mark[:, local_parent : local_parent + 1] * waves[
            local_parent : local_parent + 1, :
        ]
        live = (page_table[local_parent : local_parent + 1, :] == page_at) & (
            turn_at < path_pages[local_parent]
        )
        owned = jnp.max(live.astype(F32), 1, keepdims=True)
        page_mark = jnp.where(lane == local_parent, (1.0 - owned) * FAR, page_mark)

    def stacked(first, count):
        return jnp.concatenate(
            [packed[:, (first + at) * HD : (first + at + 1) * HD] for at in range(count)], 0
        )

    def rope(vectors, count):
        cos = jnp.concatenate([wave[:, :HD]] * count, 0)
        sin = jnp.concatenate([wave[:, HD:]] * count, 0)
        return vectors * cos + pltpu.roll(vectors, HD // 2, 1) * sin

    queries = rope(stacked(0, heads), heads)
    new_keys = rope(stacked(heads, kv_local), kv_local)
    turned = jnp.dot(
        queries, rotation, precision=lax.Precision.HIGHEST, preferred_element_type=F32
    ).astype(BF16)
    scale = 1.0 / math.sqrt(HD)
    rate = scale * math.log2(math.e)
    rows = group_size * slots
    chunk = chunk_pages * PAGE
    chunks = POOL // chunk_pages
    marks = jnp.concatenate([slot_mark.astype(BF16)] * group_size, 0)
    page_marks[...] = page_mark
    for kv_at in range(kv_local):
        query_now = queries[kv_at * rows : (kv_at + 1) * rows]
        left = jnp.concatenate([turned[kv_at * rows : (kv_at + 1) * rows], marks], 1)
        key_now = jnp.concatenate([new_keys[kv_at * slots : (kv_at + 1) * slots]] * group_size, 0)
        own_score = jnp.sum(query_now * key_now, 1, keepdims=True)
        own_row = jnp.broadcast_to(own_score, (rows, HD)).T[:1]
        span = slice(kv_at * HD, (kv_at + 1) * HD)

        def first_pass(at, best):
            pages = pl.ds(pl.multiple_of(at * chunk_pages, chunk_pages), chunk_pages)
            page_keys = kbuf[pages, :, span].reshape(chunk, HD)
            mark = jnp.broadcast_to(
                page_marks[pages, :][:, None, :], (chunk_pages, PAGE, EXT)
            ).reshape(chunk, EXT)
            now = lax.dot_general(
                jnp.concatenate([page_keys, mark.astype(BF16)], 1),
                left,
                (((1,), (1,)), ((), ())),
                preferred_element_type=F32,
            )
            scores[at] = now
            return jnp.maximum(best, jnp.max(now.reshape(chunk // 8, 8, rows), 0))

        best = lax.fori_loop(
            0, chunks, first_pass, jnp.full((8, rows), -jnp.inf, F32), unroll=unroll
        )
        top = jnp.maximum(jnp.max(best, 0, keepdims=True), own_row)
        top_rate = top * rate
        mixed[...] = jnp.zeros_like(mixed)

        def second_pass(at, sums):
            pages = pl.ds(pl.multiple_of(at * chunk_pages, chunk_pages), chunk_pages)
            weights = jnp.exp2(scores[at] * rate - top_rate)
            page_values = vbuf[pages, :, span].reshape(chunk, HD)
            mixed[...] += lax.dot_general(
                page_values,
                weights.astype(BF16),
                (((0,), (0,)), ((), ())),
                preferred_element_type=F32,
            )
            return sums + jnp.sum(weights.reshape(chunk // 8, 8, rows), 0)

        sums = lax.fori_loop(0, chunks, second_pass, jnp.zeros((8, rows), F32), unroll=unroll)
        own = jnp.exp2(own_row * rate - top_rate)
        whole = jnp.sum(sums, 0, keepdims=True) + own
        unturned = jnp.dot(
            rotation, mixed[...], precision=lax.Precision.HIGHEST, preferred_element_type=F32
        )
        value_at = (heads + kv_local + kv_at) * HD
        value_now = jnp.concatenate([packed[:, value_at : value_at + HD]] * group_size, 0)
        result = ((unturned + own * value_now.T) / whole).T.astype(BF16)
        for head in range(group_size):
            at = (kv_at * group_size + head) * HD
            out[:, at : at + HD] = result[head * slots : (head + 1) * slots]


def spread_rows(rows, order, weight, width, mine, others):
    ordered = dot32(order, rows).astype(BF16)
    share = mine.shape[0]
    for step in range(weight.shape[1] // width):
        span = slice(step * width, (step + 1) * width)
        product = dot32(ordered, weight[:, span])
        mine[:, span] = product[:share]
        for at, ref in enumerate(others):
            ref[:, span] = product[(at + 1) * share : (at + 2) * share].astype(BF16)


def mixer_kernel(slots, local_rows, chips, head_count, width, *refs):
    blocks_n = chips * CORES
    spot, codes = refs[:2]
    blocks = refs[2 : 2 + blocks_n]
    weight, mine = refs[2 + blocks_n : 4 + blocks_n]
    place = Place(spot, chips, head_count)
    sources = place.sources()
    slot_rows = onehot(codes[:, :1], column(sources, slots))
    child_rows = onehot(column(place.to_heads(), mine.shape[0]), column(sources, local_rows))
    order = dot32(child_rows, slot_rows).astype(BF16)
    rows = jnp.concatenate([ref[...] for ref in blocks], 0)
    spread_rows(rows, order, weight, width, mine, refs[4 + blocks_n :])


def lower_kernel(first, last, local_rows, chips, head_count, width, *refs):
    blocks_n = chips * CORES
    spot = refs[0]
    blocks = refs[1 : 1 + blocks_n]
    weight = refs[1 + blocks_n]
    before = None if first == 0 else refs[2 + blocks_n]
    outs = refs[(2 if first == 0 else 3) + blocks_n :]
    place = Place(spot, chips, head_count)
    share_rows = chips * CORES * local_rows // head_count
    order = onehot(column(place.to_heads(), share_rows), column(place.sources(), local_rows))
    rows = jnp.concatenate([ref[...] for ref in blocks], 0)
    ordered = dot32(order, rows).astype(BF16)
    deep = rows.shape[1]
    for step in range(weight.shape[1] // width):
        span = slice(step * width, (step + 1) * width)
        product = dot32(ordered, weight[first : first + deep, span])
        if before is not None:
            product = product + before[:, span]
        if not last:
            outs[0][:, span] = product
            continue
        outs[0][:, span] = product[:share_rows]
        for at, ref in enumerate(outs[1:]):
            ref[:, span] = product[(at + 1) * share_rows : (at + 2) * share_rows].astype(BF16)


def residual_kernel(share, mine, gain, *refs):
    received = refs[:-2]
    residual, scaled = refs[-2:]
    total = mine[...]
    for ref in received:
        total = total + ref[...].astype(F32)
    total = share[...].astype(F32) + total
    residual[...] = total
    scaled[:, :-EXT] = (total * gain[...]).astype(BF16)
    scaled[:, -EXT:] = split_lanes(jnp.sum(total * total, 1, keepdims=True))


def gate_columns(ordered, weights, first, count, width, keep, send):
    half = keep.shape[0]
    scaled = ordered[:, :-EXT]
    at = 0
    for weight in weights:
        for step in range(count // width):
            low = first + step * width
            product = dot32(scaled, weight[:, low : low + width])
            keep[:, at : at + width] = product[:half]
            send[:, at : at + width] = product[half:].astype(BF16)
            at += width


def first_gate_kernel(local_rows, chips, head_count, count, width, *refs):
    spot = refs[0]
    blocks = refs[1 : 1 + head_count]
    w_gate, w_up, keep, send, rest = refs[1 + head_count :]
    place = Place(spot, chips, head_count)
    order = onehot(
        column(place.targets(), local_rows), column(place.from_heads(), blocks[0].shape[0])
    )
    rows = jnp.concatenate([ref[...] for ref in blocks], 0)
    ordered = dot32(order, rows).astype(BF16)
    rest[...] = ordered
    half = keep.shape[0]
    keep[:, -EXT:] = ordered[:half, -EXT:].astype(F32)
    send[:, -EXT:] = ordered[half:, -EXT:]
    gate_columns(ordered, (w_gate, w_up), 0, count, width, keep, send)


def next_gate_kernel(first, count, width, ordered, w_gate, w_up, keep, send):
    gate_columns(ordered[...], (w_gate, w_up), first, count, width, keep, send)


def chip_gate_kernel(local_rows, columns, keep, got, mine, *others):
    mine[...] = keep[:local_rows] + got[:local_rows].astype(F32)
    for at, ref in enumerate(others):
        low, high = (at + 1) * local_rows, (at + 2) * local_rows
        total = keep[low:high] + got[low:high].astype(F32)
        ref[:, :columns] = total[:, :columns].astype(BF16)
        if total.shape[1] > columns:
            ref[:, columns:] = split_lanes(jnp.sum(total[:, columns:], 1, keepdims=True))


def gated(mine, received, columns, scale):
    gate = mine[:, :columns]
    up = mine[:, columns : 2 * columns]
    for ref in received:
        gate = gate + ref[:, :columns].astype(F32)
        up = up + ref[:, columns : 2 * columns].astype(F32)
    gate = gate * scale
    up = up * scale
    return (gate / (1.0 + jnp.exp(-gate)) * up).astype(BF16)


def first_activate_kernel(mine, *refs):
    received, _, out, scale_out = refs[:-3], refs[-3], refs[-2], refs[-1]
    squares = jnp.sum(mine[:, -EXT:], 1, keepdims=True)
    for ref in received:
        squares = squares + jnp.sum(ref[:, -EXT:].astype(F32), 1, keepdims=True)
    scale = lax.rsqrt(squares * (1.0 / D) + EPS)
    scale_out[...] = jnp.broadcast_to(scale, scale_out.shape)
    out[...] = gated(mine, received, out.shape[1], scale)


def next_activate_kernel(scale, mine, *refs):
    out = refs[-1]
    out[...] = gated(mine, refs[:-1], out.shape[1], scale[:, :1])


def final_kernel(residual, mine, *refs):
    received, out = refs[:-1], refs[-1]
    total = mine[...]
    for ref in received:
        total = total + ref[...].astype(F32)
    out[...] = (residual[...] + total).astype(BF16)


def local(
    hidden_in,
    input_gain,
    w_query,
    b_query,
    w_key,
    b_key,
    w_value,
    b_value,
    key_pages,
    value_pages,
    path_pages,
    page_table,
    parent_index,
    w_out,
    post_gain,
    w_gate,
    w_up,
    w_down,
):
    branch_count = lax.axis_size("branch")
    head_count = lax.axis_size("head")
    branch_pos = lax.axis_index("branch")
    head_pos = lax.axis_index("head")
    chips = branch_count // CORES
    local_rows = hidden_in.shape[0]
    all_rows = local_rows * branch_count
    share_rows = all_rows // head_count
    model_cols = w_query.shape[0]
    query_cols = w_query.shape[1]
    kv_cols = w_key.shape[1]
    kv_local = kv_cols // HD
    heads_local = query_cols // HD
    group_size = heads_local // kv_local
    slots = branch_count * CAP
    ff_local = w_gate.shape[1]
    packed_cols = query_cols + 2 * kv_cols
    spot = jnp.stack([branch_pos, head_pos]).astype(jnp.int32)
    steps = [(chip, core) for core in range(CORES) for chip in range(chips)]

    def over_branch(array, chip_step, core_step):
        pairs = []
        for source in range(branch_count):
            chip, core = source // CORES, source % CORES
            to = (chip + chip_step) % chips * CORES + (core + core_step) % CORES
            pairs.append((source, to))
        return lax.ppermute(array, "branch", pairs)

    def over_head(array, step):
        pairs = [(source, (source + step) % head_count) for source in range(head_count)]
        return lax.ppermute(array, "head", pairs)

    def gain_slice(gain):
        return lax.dynamic_slice_in_dim(gain, branch_pos * model_cols, model_cols, 0).astype(F32)[
            None
        ]

    outgoing = call(
        functools.partial(send_kernel, chips),
        [((local_rows, model_cols + EXT), BF16)] * branch_count,
        ["hbm", "hbm"],
        [pltpu.VMEM((1, local_rows), jnp.int32), pltpu.SemaphoreType.DMA((branch_count + 1,))],
        hidden_in,
        parent_index[None],
        limit=SEND_LIMIT,
        near=True,
    )
    hidden_blocks = [outgoing[0]]
    for block, (chip, core) in zip(outgoing[1:], steps[1:]):
        hidden_blocks.append(over_branch(block, chip, core))
    wq, wk, wv = fetch([w_query, w_key, w_value], outgoing[0], 44 * MIB)
    keep, send, share, codes = call(
        functools.partial(qkv_kernel, slots, chips, head_count, 512),
        [
            ((chips * slots, packed_cols + EXT), F32),
            ((chips * slots, packed_cols + EXT), F32),
            ((share_rows, model_cols), BF16),
            ((all_rows, EXT), F32),
        ],
        ["smem"] + ["vmem"] * (branch_count + 4),
        [],
        spot,
        *hidden_blocks,
        gain_slice(input_gain),
        wq,
        wk,
        wv,
        flops=2 * all_rows * model_cols * packed_cols,
    )
    got = over_branch(send, 0, 1)
    mine, *others = call(
        functools.partial(chip_sum_kernel, slots),
        [((slots, packed_cols + EXT), F32)]
        + [((slots, packed_cols + EXT), BF16)] * (chips - 1),
        ["vmem"] * 2,
        [],
        keep,
        got,
    )
    received = [over_branch(other, at + 1, 0) for at, other in enumerate(others)]
    keys, values = fetch([key_pages, value_pages], others[0])

    freqs = THETA ** (-(jnp.arange(HD // 2, dtype=F32) * 2.0 / HD))
    angle = (path_pages.astype(F32) * PAGE)[:, None] * freqs
    cosine, sine = jnp.cos(angle), jnp.sin(angle)
    waves = jnp.concatenate([cosine, cosine, -sine, sine], 1)
    rows = group_size * slots
    chunk_pages, unroll = (16, 2) if rows <= 512 else (4, 1)
    score_bytes = 4 * rows * POOL * PAGE
    (attention,) = call(
        functools.partial(attend_kernel, kv_local, group_size, chunk_pages, unroll, chips - 1),
        [((slots, query_cols), BF16)],
        ["smem"] * 2 + ["vmem"] * (chips + 9),
        [
            pltpu.VMEM((POOL // chunk_pages, chunk_pages * PAGE, rows), F32),
            pltpu.VMEM((HD, rows), F32),
            pltpu.VMEM((POOL, EXT), F32),
        ],
        spot,
        path_pages,
        mine,
        *received,
        b_query[None],
        b_key[None],
        b_value[None],
        waves,
        codes,
        page_table,
        jnp.asarray(hadamard(HD)),
        keys,
        values,
        limit=score_bytes + SPARE + SPARE // 2,
        flops=4 * kv_cols * rows * POOL * PAGE,
    )

    def gather_branch(array):
        near = [array] + [over_branch(array, chip, 0) for chip in range(1, chips)]
        return near + [over_branch(block, 0, 1) for block in near]

    gathered = gather_branch(attention)
    (w_out_near,) = fetch([w_out], attention)
    out_width = block_width(model_cols, 512)
    mixer, *others = call(
        functools.partial(mixer_kernel, slots, local_rows, chips, head_count, out_width),
        [((share_rows, model_cols), F32)] + [((share_rows, model_cols), BF16)] * (head_count - 1),
        ["smem"] + ["vmem"] * (branch_count + 2),
        [],
        spot,
        codes,
        *gathered,
        w_out_near,
        flops=2 * all_rows * w_out.size,
    )
    received = [over_head(other, at + 1) for at, other in enumerate(others)]
    (w_gate_near,) = fetch([w_gate], mixer)
    residual, scaled = call(
        residual_kernel,
        [((share_rows, model_cols), F32), ((share_rows, model_cols + EXT), BF16)],
        ["vmem"] * (head_count + 2),
        [],
        share,
        mixer,
        gain_slice(post_gain),
        *received,
    )
    scaled_blocks = [scaled] + [over_head(scaled, step) for step in range(1, head_count)]
    (w_up_near,) = fetch([w_up], scaled)
    tiles = ff_local // 128
    cuts = [0, (tiles + 1) // 2 * 128, ff_local]
    counts = [high - low for low, high in zip(cuts, cuts[1:])]

    def gate_outs(extra):
        return [((chips * local_rows, extra), F32), ((chips * local_rows, extra), BF16)]

    keep, send, ordered = call(
        functools.partial(
            first_gate_kernel,
            local_rows,
            chips,
            head_count,
            counts[0],
            block_width(counts[0], 768),
        ),
        gate_outs(2 * counts[0] + EXT) + [((all_rows, model_cols + EXT), BF16)],
        ["smem"] + ["vmem"] * (head_count + 2),
        [],
        spot,
        *scaled_blocks,
        w_gate_near,
        w_up_near,
        flops=4 * all_rows * model_cols * counts[0],
    )
    parts = [(keep, over_branch(send, 0, 1))]
    keep, send = call(
        functools.partial(next_gate_kernel, cuts[1], counts[1], block_width(counts[1], 768)),
        gate_outs(2 * counts[1]),
        ["vmem"] * 3,
        [],
        ordered,
        w_gate_near,
        w_up_near,
        flops=4 * all_rows * model_cols * counts[1],
    )
    parts.append((keep, over_branch(send, 0, 1)))
    sums = []
    for (keep, got), count in zip(parts, counts):
        wide = keep.shape[1]
        mine, *others = call(
            functools.partial(chip_gate_kernel, local_rows, 2 * count),
            [((local_rows, wide), F32)] + [((local_rows, wide), BF16)] * (chips - 1),
            ["vmem"] * 2,
            [],
            keep,
            got,
        )
        sums.append((mine, [over_branch(other, at + 1, 0) for at, other in enumerate(others)], others))
    (w_down_near,) = fetch([w_down], sums[1][2][0], 32 * MIB)
    activated, scale = call(
        first_activate_kernel,
        [((local_rows, counts[0]), BF16), ((local_rows, EXT), F32)],
        ["vmem"] * chips + ["any"],
        [],
        sums[0][0],
        *sums[0][1],
        w_down_near,
    )
    gathered = gather_branch(activated)
    (activated,) = call(
        next_activate_kernel,
        [((local_rows, counts[1]), BF16)],
        ["vmem"] * (chips + 1),
        [],
        scale,
        sums[1][0],
        *sums[1][1],
    )
    gathered_next = gather_branch(activated)
    (partial,) = call(
        functools.partial(lower_kernel, 0, False, local_rows, chips, head_count, out_width),
        [((all_rows, model_cols), F32)],
        ["smem"] + ["vmem"] * (branch_count + 1),
        [],
        spot,
        *gathered,
        w_down_near,
        flops=2 * all_rows * model_cols * counts[0],
    )
    lowered, *others = call(
        functools.partial(lower_kernel, cuts[1], True, local_rows, chips, head_count, out_width),
        [((share_rows, model_cols), F32)] + [((share_rows, model_cols), BF16)] * (head_count - 1),
        ["smem"] + ["vmem"] * (branch_count + 2),
        [],
        spot,
        *gathered_next,
        w_down_near,
        partial,
        flops=2 * all_rows * model_cols * counts[1],
    )
    received = [over_head(other, at + 1) for at, other in enumerate(others)]
    (final,) = call(
        final_kernel,
        [((share_rows, model_cols), BF16)],
        ["vmem"] * (head_count + 1),
        [],
        residual,
        lowered,
        *received,
    )
    return final


def solution(mesh):
    placed = (
        P(("groups", "branch"), None),
        P(),
        P("branch", "head"),
        P("head"),
        P("branch", "head"),
        P("head"),
        P("branch", "head"),
        P("head"),
        P(("groups", "branch"), None, "head"),
        P(("groups", "branch"), None, "head"),
        P(("groups", "branch")),
        P(("groups", "branch"), None),
        P(("groups", "branch")),
        P("head", "branch"),
        P(),
        P("branch", "head"),
        P("branch", "head"),
        P("head", "branch"),
    )
    return jax.shard_map(
        local,
        mesh=mesh,
        in_specs=placed,
        out_specs=P(("groups", "head"), "branch"),
        check_vma=False,
    )
```

```python
import functools
import math

import jax
import jax.numpy as jnp
import numpy as np
from jax import lax
from jax.experimental import pallas as pl
from jax.experimental.pallas import tpu as pltpu
from jax.sharding import PartitionSpec as P

D = 8192
HD = 128
PAGE = 128
MAXP = 32
POOL = 64
P_DEV = 4
CAP = 8
EXT = 128
CORES = 2

EPS = 1e-06
THETA = 1000000.0
FAR = -1e30
MIB = 1024 * 1024
SPARE = 10 * MIB
SEND_LIMIT = 63 * MIB

F32 = jnp.float32
BF16 = jnp.bfloat16


def hadamard(order_size):
    index = np.arange(order_size)
    common = index[:, None] & index[None, :]
    parity = np.zeros((order_size, order_size), np.int64)
    for bit_level in range(order_size.bit_length() - 1):
        parity = parity ^ (common >> bit_level & 1)
    return ((1 - 2 * parity).astype(np.float32) / np.float32(math.sqrt(order_size))).astype(
        np.float32
    )


SPACES = {"vmem": pltpu.VMEM, "hbm": pltpu.HBM, "any": pl.ANY, "smem": pltpu.SMEM}


def call(kernel, outs, in_spaces, scratch, *args, limit=SPARE, flops=0, moved=0, near=False):
    return pl.pallas_call(
        kernel,
        out_shape=[
            pltpu.VMEM(shape, kind) if near else jax.ShapeDtypeStruct(shape, kind)
            for shape, kind in outs
        ],
        in_specs=[pl.BlockSpec(memory_space=SPACES[space]) for space in in_spaces],
        out_specs=[pl.BlockSpec(memory_space=pltpu.VMEM) for _ in outs],
        scratch_shapes=scratch,
        compiler_params=pltpu.CompilerParams(vmem_limit_bytes=limit),
        cost_estimate=pl.CostEstimate(flops=flops, bytes_accessed=moved, transcendentals=0),
    )(*args)


def fetch_kernel(count, *refs):
    sources, targets, sems = refs[:count], refs[-1 - count : -1], refs[-1]
    copies = [
        pltpu.make_async_copy(source, target, sems.at[at])
        for at, (source, target) in enumerate(zip(sources, targets))
    ]
    for copy in copies:
        copy.start()
    for copy in copies:
        copy.wait()


def fetch(arrays, after, limit=2 * MIB):
    size = sum(array.size * array.dtype.itemsize for array in arrays)
    return pl.pallas_call(
        functools.partial(fetch_kernel, len(arrays)),
        out_shape=[pltpu.VMEM(array.shape, array.dtype) for array in arrays],
        in_specs=[pl.BlockSpec(memory_space=pltpu.HBM)] * len(arrays)
        + [pl.BlockSpec(memory_space=pl.ANY)],
        out_specs=[pl.BlockSpec(memory_space=pltpu.VMEM)] * len(arrays),
        scratch_shapes=[pltpu.SemaphoreType.DMA((len(arrays),))],
        compiler_params=pltpu.CompilerParams(vmem_limit_bytes=limit),
        cost_estimate=pl.CostEstimate(flops=0, bytes_accessed=2 * size, transcendentals=0),
    )(*arrays, after)


def block_width(columns, most):
    best = 128
    for width in range(128, most + 1, 128):
        if columns % width == 0:
            best = width
    return best


class Place:
    def __init__(self, spot, chips, head_count):
        self.chips = chips
        self.head_count = head_count
        self.branch, self.head = spot[0], spot[1]
        self.chip, self.core = self.branch // CORES, self.branch % CORES
        self.steps = [(chip, core) for core in range(CORES) for chip in range(chips)]

    def targets(self):
        return [
            (self.chip + chip) % self.chips * CORES + (self.core + core) % CORES
            for chip, core in self.steps
        ]

    def sources(self):
        return [
            (self.chip + self.chips - chip) % self.chips * CORES + (self.core + core) % CORES
            for chip, core in self.steps
        ]

    def to_heads(self):
        return [(self.head + step) % self.head_count for step in range(self.head_count)]

    def from_heads(self):
        return [
            (self.head + self.head_count - step) % self.head_count
            for step in range(self.head_count)
        ]


def column(devices, length):
    iota = lax.broadcasted_iota(jnp.int32, (length, 1), 0)
    return jnp.concatenate([iota + device * length for device in devices], 0).astype(F32)


def to_row(values):
    size = values.shape[0]
    row_at = lax.broadcasted_iota(jnp.int32, (size, size), 0)
    col_at = lax.broadcasted_iota(jnp.int32, (size, size), 1)
    return jnp.sum(jnp.where(row_at == col_at, values, 0.0), 0, keepdims=True)


def onehot(rows, columns):
    return (rows == to_row(columns)).astype(BF16)


def split_lanes(total):
    rows = total.shape[0]
    high = total.astype(BF16).astype(F32)
    rest = total - high
    middle = rest.astype(BF16).astype(F32)
    low = rest - middle
    lane = lax.broadcasted_iota(jnp.int32, (rows, EXT), 1)
    zero = jnp.zeros((rows, EXT), F32)
    return jnp.where(
        lane == 0, high, jnp.where(lane == 1, middle, jnp.where(lane == 2, low, zero))
    ).astype(BF16)


def dot32(left, right):
    return jnp.dot(left, right, preferred_element_type=F32)


def send_kernel(chips, hidden, parents, *refs):
    blocks, (listed, sems) = refs[:-2], refs[-2:]
    place = Place((lax.axis_index("branch"), 0), chips, 1)
    length, width = hidden.shape[0], blocks[0].shape[1] - EXT
    copies = [pltpu.make_async_copy(parents, listed, sems.at[0])]
    for at, (ref, device) in enumerate(zip(blocks, place.targets())):
        source = hidden.at[:, pl.ds(pl.multiple_of(device * width, width), width)]
        copies.append(pltpu.make_async_copy(source, ref.at[:, :width], sems.at[at + 1]))
    for copy in copies:
        copy.start()
    copies[0].wait()
    row_at = lax.broadcasted_iota(jnp.int32, (length, length), 0)
    col_at = lax.broadcasted_iota(jnp.int32, (length, length), 1)
    turned = jnp.sum(jnp.where(row_at == col_at, listed[...].astype(F32), 0.0), 1, keepdims=True)
    mark = jnp.broadcast_to(turned, (length, EXT)).astype(BF16)
    for ref in blocks:
        ref[:, width:] = mark
    for copy in copies[1:]:
        copy.wait()


def qkv_kernel(slots, chips, head_count, width, *refs):
    spot = refs[0]
    blocks_n = chips * CORES
    blocks = refs[1 : 1 + blocks_n]
    gain, wq, wk, wv, keep, send, share, codes = refs[1 + blocks_n :]
    place = Place(spot, chips, head_count)
    model_cols = gain.shape[1]
    length = blocks[0].shape[0]
    rows = jnp.concatenate([ref[:, :model_cols] for ref in blocks], 0)
    parent = jnp.concatenate([ref[:, model_cols:] for ref in blocks], 0)[:, :1].astype(F32)
    dest = jnp.floor(parent * (1.0 / P_DEV))
    order = column(place.sources(), length)
    order_row = to_row(order)
    same = (dest == to_row(dest)) & (order_row < order)
    code = dest * slots + jnp.sum(same.astype(F32), 1, keepdims=True)
    lane = lax.broadcasted_iota(jnp.int32, codes.shape, 1)
    codes[...] = jnp.where(lane == 0, code, parent)
    placing = onehot(column(place.targets(), slots), code)
    own = column([place.head], share.shape[0])
    share[...] = dot32((own == order_row).astype(BF16), rows).astype(BF16)
    placed = dot32(placing, rows)
    squares = jnp.sum(placed * placed, 1, keepdims=True)
    scaled = (placed * gain[...]).astype(BF16)
    half = keep.shape[0]
    total_cols = keep.shape[1] - EXT
    keep[:, total_cols:] = jnp.broadcast_to(squares[:half], (half, EXT))
    send[:, total_cols:] = jnp.broadcast_to(squares[half:], (half, EXT))
    at = 0
    for weight in (wq, wk, wv):
        wide = block_width(weight.shape[1], width)
        for step in range(weight.shape[1] // wide):
            product = dot32(scaled, weight[:, step * wide : (step + 1) * wide])
            keep[:, at : at + wide] = product[:half]
            send[:, at : at + wide] = product[half:]
            at += wide


def chip_sum_kernel(slots, keep, got, mine, *others):
    mine[...] = keep[:slots] + got[:slots]
    for at, ref in enumerate(others):
        low, high = (at + 1) * slots, (at + 2) * slots
        total = keep[low:high] + got[low:high]
        ref[:, :-EXT] = total[:, :-EXT].astype(BF16)
        ref[:, -EXT:] = split_lanes(total[:, -EXT:][:, :1])


def marks_kernel(
    slots,
    local_rows,
    chips,
    head_count,
    spot,
    path_pages,
    page_table,
    codes,
    waves,
    bq,
    bk,
    bv,
    _,
    wave_out,
    slot_out,
    page_out,
    bias_out,
    mixer_order,
    gate_order,
    lower_order,
):
    place = Place(spot, chips, head_count)
    share_rows = chips * CORES * local_rows // head_count
    code, parent = codes[:, :1], codes[:, 1:2]
    lane = lax.broadcasted_iota(jnp.int32, (1, EXT), 1).astype(F32)
    parent_at = (parent - jnp.floor(parent * (1.0 / P_DEV)) * P_DEV == lane).astype(BF16)
    slot_mark = dot32(onehot(column([spot[0]], slots), code), parent_at)
    wave = jnp.zeros((slots, 2 * HD), F32)
    page_at = lax.broadcasted_iota(jnp.int32, (POOL, MAXP), 0)
    turn_at = lax.broadcasted_iota(jnp.int32, (POOL, MAXP), 1)
    page_mark = jnp.zeros((POOL, EXT), F32)
    for local_parent in range(P_DEV):
        wave = wave + slot_mark[:, local_parent : local_parent + 1] * waves[
            local_parent : local_parent + 1, :
        ]
        live = (page_table[local_parent : local_parent + 1, :] == page_at) & (
            turn_at < path_pages[local_parent]
        )
        owned = jnp.max(live.astype(F32), 1, keepdims=True)
        page_mark = jnp.where(lane == local_parent, (1.0 - owned) * FAR, page_mark)
    wave_out[...] = wave
    slot_out[...] = slot_mark.astype(BF16)
    page_out[...] = page_mark
    bias_out[...] = jnp.concatenate([ref[...].astype(F32) for ref in (bq, bk, bv)], 1)
    child_at = column(place.sources(), local_rows)
    lower = onehot(column(place.to_heads(), share_rows), child_at)
    lower_order[...] = lower
    slot_rows = onehot(code, column(place.sources(), slots))
    mixer_order[...] = dot32(lower, slot_rows).astype(BF16)
    gate_order[...] = onehot(
        column(place.targets(), local_rows), column(place.from_heads(), share_rows)
    )


def attend_kernel(kv_local, group_size, chunk_pages, unroll, received_n, *refs):
    mine = refs[0]
    received = refs[1 : 1 + received_n]
    bias, wave, slot_mark, page_marks, turn, kbuf, vbuf = refs[1 + received_n : 8 + received_n]
    out, scores, mixed = refs[8 + received_n :]
    slots = mine.shape[0]
    squares = mine[:, -EXT:][:, :1]
    total = mine[:, :-EXT]
    for ref in received:
        total = total + ref[:, :-EXT].astype(F32)
        squares = squares + jnp.sum(ref[:, -EXT:].astype(F32), 1, keepdims=True)
    packed = (total * lax.rsqrt(squares * (1.0 / D) + EPS) + bias[...]).astype(BF16).astype(F32)
    heads = kv_local * group_size
    rotation = turn[...]
    def stacked(first, count):
        return jnp.concatenate(
            [packed[:, (first + at) * HD : (first + at + 1) * HD] for at in range(count)], 0
        )

    def rope(vectors, count):
        cos = jnp.concatenate([wave[:, :HD]] * count, 0)
        sin = jnp.concatenate([wave[:, HD:]] * count, 0)
        return vectors * cos + pltpu.roll(vectors, HD // 2, 1) * sin

    queries = rope(stacked(0, heads), heads)
    new_keys = rope(stacked(heads, kv_local), kv_local)
    turned = jnp.dot(
        queries, rotation, precision=lax.Precision.HIGHEST, preferred_element_type=F32
    ).astype(BF16)
    scale = 1.0 / math.sqrt(HD)
    rate = scale * math.log2(math.e)
    rows = group_size * slots
    chunk = chunk_pages * PAGE
    chunks = POOL // chunk_pages
    marks = jnp.concatenate([slot_mark[...]] * group_size, 0)
    for kv_at in range(kv_local):
        query_now = queries[kv_at * rows : (kv_at + 1) * rows]
        left = jnp.concatenate([turned[kv_at * rows : (kv_at + 1) * rows], marks], 1)
        key_now = jnp.concatenate([new_keys[kv_at * slots : (kv_at + 1) * slots]] * group_size, 0)
        own_score = jnp.sum(query_now * key_now, 1, keepdims=True)
        own_row = jnp.broadcast_to(own_score, (rows, HD)).T[:1]
        span = slice(kv_at * HD, (kv_at + 1) * HD)

        def first_pass(at, best):
            pages = pl.ds(pl.multiple_of(at * chunk_pages, chunk_pages), chunk_pages)
            page_keys = kbuf[pages, :, span].reshape(chunk, HD)
            mark = jnp.broadcast_to(
                page_marks[pages, :][:, None, :], (chunk_pages, PAGE, EXT)
            ).reshape(chunk, EXT)
            now = lax.dot_general(
                jnp.concatenate([page_keys, mark.astype(BF16)], 1),
                left,
                (((1,), (1,)), ((), ())),
                preferred_element_type=F32,
            )
            scores[at] = now
            return jnp.maximum(best, jnp.max(now.reshape(chunk // 8, 8, rows), 0))

        best = lax.fori_loop(
            0, chunks, first_pass, jnp.full((8, rows), -jnp.inf, F32), unroll=unroll
        )
        top = jnp.maximum(jnp.max(best, 0, keepdims=True), own_row)
        top_rate = top * rate
        mixed[...] = jnp.zeros_like(mixed)

        def second_pass(at, sums):
            pages = pl.ds(pl.multiple_of(at * chunk_pages, chunk_pages), chunk_pages)
            weights = jnp.exp2(scores[at] * rate - top_rate)
            page_values = vbuf[pages, :, span].reshape(chunk, HD)
            mixed[...] += lax.dot_general(
                page_values,
                weights.astype(BF16),
                (((0,), (0,)), ((), ())),
                preferred_element_type=F32,
            )
            return sums + jnp.sum(weights.reshape(chunk // 8, 8, rows), 0)

        sums = lax.fori_loop(0, chunks, second_pass, jnp.zeros((8, rows), F32), unroll=unroll)
        own = jnp.exp2(own_row * rate - top_rate)
        whole = jnp.sum(sums, 0, keepdims=True) + own
        unturned = jnp.dot(
            rotation, mixed[...], precision=lax.Precision.HIGHEST, preferred_element_type=F32
        )
        value_at = (heads + kv_local + kv_at) * HD
        value_now = jnp.concatenate([packed[:, value_at : value_at + HD]] * group_size, 0)
        result = ((unturned + own * value_now.T) / whole).T.astype(BF16)
        for head in range(group_size):
            at = (kv_at * group_size + head) * HD
            out[:, at : at + HD] = result[head * slots : (head + 1) * slots]


def spread_rows(rows, order, weight, width, mine, others):
    ordered = dot32(order, rows).astype(BF16)
    share = mine.shape[0]
    for step in range(weight.shape[1] // width):
        span = slice(step * width, (step + 1) * width)
        product = dot32(ordered, weight[:, span])
        mine[:, span] = product[:share]
        for at, ref in enumerate(others):
            ref[:, span] = product[(at + 1) * share : (at + 2) * share].astype(BF16)


def mixer_kernel(blocks_n, width, order, *refs):
    blocks = refs[:blocks_n]
    weight, mine = refs[blocks_n : 2 + blocks_n]
    rows = jnp.concatenate([ref[...] for ref in blocks], 0)
    spread_rows(rows, order[...], weight, width, mine, refs[2 + blocks_n :])


def lower_kernel(first, last, blocks_n, share_rows, width, *refs):
    order = refs[0]
    blocks = refs[1 : 1 + blocks_n]
    weight = refs[1 + blocks_n]
    before = None if first == 0 else refs[2 + blocks_n]
    outs = refs[(2 if first == 0 else 3) + blocks_n :]
    rows = jnp.concatenate([ref[...] for ref in blocks], 0)
    ordered = dot32(order[...], rows).astype(BF16)
    deep = rows.shape[1]
    for step in range(weight.shape[1] // width):
        span = slice(step * width, (step + 1) * width)
        product = dot32(ordered, weight[first : first + deep, span])
        if before is not None:
            product = product + before[:, span]
        if not last:
            outs[0][:, span] = product
            continue
        outs[0][:, span] = product[:share_rows]
        for at, ref in enumerate(outs[1:]):
            ref[:, span] = product[(at + 1) * share_rows : (at + 2) * share_rows].astype(BF16)


def residual_kernel(share, mine, gain, *refs):
    received = refs[:-2]
    residual, scaled = refs[-2:]
    total = mine[...]
    for ref in received:
        total = total + ref[...].astype(F32)
    total = share[...].astype(F32) + total
    residual[...] = total
    scaled[:, :-EXT] = (total * gain[...]).astype(BF16)
    scaled[:, -EXT:] = split_lanes(jnp.sum(total * total, 1, keepdims=True))


def gate_columns(ordered, weights, first, count, width, keep, send):
    half = keep.shape[0]
    scaled = ordered[:, :-EXT]
    at = 0
    for weight in weights:
        for step in range(count // width):
            low = first + step * width
            product = dot32(scaled, weight[:, low : low + width])
            keep[:, at : at + width] = product[:half]
            send[:, at : at + width] = product[half:].astype(BF16)
            at += width


def first_gate_kernel(head_count, count, width, *refs):
    order = refs[0]
    blocks = refs[1 : 1 + head_count]
    w_gate, w_up, keep, send, rest = refs[1 + head_count :]
    rows = jnp.concatenate([ref[...] for ref in blocks], 0)
    ordered = dot32(order[...], rows).astype(BF16)
    rest[...] = ordered
    half = keep.shape[0]
    keep[:, -EXT:] = ordered[:half, -EXT:].astype(F32)
    send[:, -EXT:] = ordered[half:, -EXT:]
    gate_columns(ordered, (w_gate, w_up), 0, count, width, keep, send)


def next_gate_kernel(first, count, width, ordered, w_gate, w_up, keep, send):
    gate_columns(ordered[...], (w_gate, w_up), first, count, width, keep, send)


def chip_gate_kernel(local_rows, columns, keep, got, mine, *others):
    mine[...] = keep[:local_rows] + got[:local_rows].astype(F32)
    for at, ref in enumerate(others):
        low, high = (at + 1) * local_rows, (at + 2) * local_rows
        total = keep[low:high] + got[low:high].astype(F32)
        ref[:, :columns] = total[:, :columns].astype(BF16)
        if total.shape[1] > columns:
            ref[:, columns:] = split_lanes(jnp.sum(total[:, columns:], 1, keepdims=True))


def gated(mine, received, columns, scale):
    gate = mine[:, :columns]
    up = mine[:, columns : 2 * columns]
    for ref in received:
        gate = gate + ref[:, :columns].astype(F32)
        up = up + ref[:, columns : 2 * columns].astype(F32)
    gate = gate * scale
    up = up * scale
    return (gate / (1.0 + jnp.exp(-gate)) * up).astype(BF16)


def first_activate_kernel(mine, *refs):
    received, _, out, scale_out = refs[:-3], refs[-3], refs[-2], refs[-1]
    squares = jnp.sum(mine[:, -EXT:], 1, keepdims=True)
    for ref in received:
        squares = squares + jnp.sum(ref[:, -EXT:].astype(F32), 1, keepdims=True)
    scale = lax.rsqrt(squares * (1.0 / D) + EPS)
    scale_out[...] = jnp.broadcast_to(scale, scale_out.shape)
    out[...] = gated(mine, received, out.shape[1], scale)


def next_activate_kernel(scale, mine, *refs):
    out = refs[-1]
    out[...] = gated(mine, refs[:-1], out.shape[1], scale[:, :1])


def final_kernel(residual, mine, *refs):
    received, out = refs[:-1], refs[-1]
    total = mine[...]
    for ref in received:
        total = total + ref[...].astype(F32)
    out[...] = (residual[...] + total).astype(BF16)


def local(
    hidden_in,
    input_gain,
    w_query,
    b_query,
    w_key,
    b_key,
    w_value,
    b_value,
    key_pages,
    value_pages,
    path_pages,
    page_table,
    parent_index,
    w_out,
    post_gain,
    w_gate,
    w_up,
    w_down,
):
    branch_count = lax.axis_size("branch")
    head_count = lax.axis_size("head")
    branch_pos = lax.axis_index("branch")
    head_pos = lax.axis_index("head")
    chips = branch_count // CORES
    local_rows = hidden_in.shape[0]
    all_rows = local_rows * branch_count
    share_rows = all_rows // head_count
    model_cols = w_query.shape[0]
    query_cols = w_query.shape[1]
    kv_cols = w_key.shape[1]
    kv_local = kv_cols // HD
    heads_local = query_cols // HD
    group_size = heads_local // kv_local
    slots = branch_count * CAP
    ff_local = w_gate.shape[1]
    packed_cols = query_cols + 2 * kv_cols
    spot = jnp.stack([branch_pos, head_pos]).astype(jnp.int32)
    steps = [(chip, core) for core in range(CORES) for chip in range(chips)]

    def over_branch(array, chip_step, core_step):
        pairs = []
        for source in range(branch_count):
            chip, core = source // CORES, source % CORES
            to = (chip + chip_step) % chips * CORES + (core + core_step) % CORES
            pairs.append((source, to))
        return lax.ppermute(array, "branch", pairs)

    def over_head(array, step):
        pairs = [(source, (source + step) % head_count) for source in range(head_count)]
        return lax.ppermute(array, "head", pairs)

    def gain_slice(gain):
        return lax.dynamic_slice_in_dim(gain, branch_pos * model_cols, model_cols, 0).astype(F32)[
            None
        ]

    outgoing = call(
        functools.partial(send_kernel, chips),
        [((local_rows, model_cols + EXT), BF16)] * branch_count,
        ["hbm", "hbm"],
        [pltpu.VMEM((1, local_rows), jnp.int32), pltpu.SemaphoreType.DMA((branch_count + 1,))],
        hidden_in,
        parent_index[None],
        limit=SEND_LIMIT,
        near=True,
    )
    hidden_blocks = [outgoing[0]]
    for block, (chip, core) in zip(outgoing[1:], steps[1:]):
        hidden_blocks.append(over_branch(block, chip, core))
    wq, wk, wv = fetch([w_query, w_key, w_value], outgoing[0], 44 * MIB)
    keep, send, share, codes = call(
        functools.partial(qkv_kernel, slots, chips, head_count, 512),
        [
            ((chips * slots, packed_cols + EXT), F32),
            ((chips * slots, packed_cols + EXT), F32),
            ((share_rows, model_cols), BF16),
            ((all_rows, EXT), F32),
        ],
        ["smem"] + ["vmem"] * (branch_count + 4),
        [],
        spot,
        *hidden_blocks,
        gain_slice(input_gain),
        wq,
        wk,
        wv,
        flops=2 * all_rows * model_cols * packed_cols,
    )
    got = over_branch(send, 0, 1)
    mine, *others = call(
        functools.partial(chip_sum_kernel, slots),
        [((slots, packed_cols + EXT), F32)]
        + [((slots, packed_cols + EXT), BF16)] * (chips - 1),
        ["vmem"] * 2,
        [],
        keep,
        got,
    )
    received = [over_branch(other, at + 1, 0) for at, other in enumerate(others)]
    keys, values = fetch([key_pages, value_pages], others[0])

    freqs = THETA ** (-(jnp.arange(HD // 2, dtype=F32) * 2.0 / HD))
    angle = (path_pages.astype(F32) * PAGE)[:, None] * freqs
    cosine, sine = jnp.cos(angle), jnp.sin(angle)
    waves = jnp.concatenate([cosine, cosine, -sine, sine], 1)
    order_out = ((all_rows, all_rows), BF16)
    wave, slot_mark, page_mark, biases, mixer_order, gate_order, lower_order = call(
        functools.partial(marks_kernel, slots, local_rows, chips, head_count),
        [
            ((slots, 2 * HD), F32),
            ((slots, EXT), BF16),
            ((POOL, EXT), F32),
            ((1, packed_cols), F32),
            ((all_rows, slots * branch_count), BF16),
            order_out,
            order_out,
        ],
        ["smem"] * 2 + ["vmem"] * 6 + ["any"],
        [],
        spot,
        path_pages,
        page_table,
        codes,
        waves,
        b_query[None],
        b_key[None],
        b_value[None],
        others[0],
        moved=MIB,
    )
    rows = group_size * slots
    chunk_pages, unroll = (16, 2) if rows <= 512 else (4, 1)
    score_bytes = 4 * rows * POOL * PAGE
    (attention,) = call(
        functools.partial(attend_kernel, kv_local, group_size, chunk_pages, unroll, chips - 1),
        [((slots, query_cols), BF16)],
        ["vmem"] * (chips + 7),
        [
            pltpu.VMEM((POOL // chunk_pages, chunk_pages * PAGE, rows), F32),
            pltpu.VMEM((HD, rows), F32),
        ],
        mine,
        *received,
        biases,
        wave,
        slot_mark,
        page_mark,
        jnp.asarray(hadamard(HD)),
        keys,
        values,
        limit=score_bytes + SPARE + SPARE // 2,
        flops=4 * kv_cols * rows * POOL * PAGE,
    )

    def gather_branch(array):
        near = [array] + [over_branch(array, chip, 0) for chip in range(1, chips)]
        return near + [over_branch(block, 0, 1) for block in near]

    gathered = gather_branch(attention)
    (w_out_near,) = fetch([w_out], attention)
    out_width = block_width(model_cols, 512)
    mixer, *others = call(
        functools.partial(mixer_kernel, branch_count, out_width),
        [((share_rows, model_cols), F32)] + [((share_rows, model_cols), BF16)] * (head_count - 1),
        ["vmem"] * (branch_count + 2),
        [],
        mixer_order,
        *gathered,
        w_out_near,
        flops=2 * all_rows * w_out.size,
    )
    received = [over_head(other, at + 1) for at, other in enumerate(others)]
    (w_gate_near,) = fetch([w_gate], mixer)
    residual, scaled = call(
        residual_kernel,
        [((share_rows, model_cols), F32), ((share_rows, model_cols + EXT), BF16)],
        ["vmem"] * (head_count + 2),
        [],
        share,
        mixer,
        gain_slice(post_gain),
        *received,
    )
    scaled_blocks = [scaled] + [over_head(scaled, step) for step in range(1, head_count)]
    (w_up_near,) = fetch([w_up], scaled)
    tiles = ff_local // 128
    cuts = [0, (tiles + 1) // 2 * 128, ff_local]
    counts = [high - low for low, high in zip(cuts, cuts[1:])]

    def gate_outs(extra):
        return [((chips * local_rows, extra), F32), ((chips * local_rows, extra), BF16)]

    keep, send, ordered = call(
        functools.partial(
            first_gate_kernel,
            head_count,
            counts[0],
            block_width(counts[0], 768),
        ),
        gate_outs(2 * counts[0] + EXT) + [((all_rows, model_cols + EXT), BF16)],
        ["vmem"] * (head_count + 3),
        [],
        gate_order,
        *scaled_blocks,
        w_gate_near,
        w_up_near,
        flops=4 * all_rows * model_cols * counts[0],
    )
    parts = [(keep, over_branch(send, 0, 1))]
    keep, send = call(
        functools.partial(next_gate_kernel, cuts[1], counts[1], block_width(counts[1], 768)),
        gate_outs(2 * counts[1]),
        ["vmem"] * 3,
        [],
        ordered,
        w_gate_near,
        w_up_near,
        flops=4 * all_rows * model_cols * counts[1],
    )
    parts.append((keep, over_branch(send, 0, 1)))
    sums = []
    for (keep, got), count in zip(parts, counts):
        wide = keep.shape[1]
        mine, *others = call(
            functools.partial(chip_gate_kernel, local_rows, 2 * count),
            [((local_rows, wide), F32)] + [((local_rows, wide), BF16)] * (chips - 1),
            ["vmem"] * 2,
            [],
            keep,
            got,
        )
        sums.append((mine, [over_branch(other, at + 1, 0) for at, other in enumerate(others)], others))
    (w_down_near,) = fetch([w_down], sums[1][2][0], 32 * MIB)
    activated, scale = call(
        first_activate_kernel,
        [((local_rows, counts[0]), BF16), ((local_rows, EXT), F32)],
        ["vmem"] * chips + ["any"],
        [],
        sums[0][0],
        *sums[0][1],
        w_down_near,
    )
    gathered = gather_branch(activated)
    (activated,) = call(
        next_activate_kernel,
        [((local_rows, counts[1]), BF16)],
        ["vmem"] * (chips + 1),
        [],
        scale,
        sums[1][0],
        *sums[1][1],
    )
    gathered_next = gather_branch(activated)
    (partial,) = call(
        functools.partial(lower_kernel, 0, False, branch_count, share_rows, out_width),
        [((all_rows, model_cols), F32)],
        ["vmem"] * (branch_count + 2),
        [],
        lower_order,
        *gathered,
        w_down_near,
        flops=2 * all_rows * model_cols * counts[0],
    )
    lowered, *others = call(
        functools.partial(lower_kernel, cuts[1], True, branch_count, share_rows, out_width),
        [((share_rows, model_cols), F32)] + [((share_rows, model_cols), BF16)] * (head_count - 1),
        ["vmem"] * (branch_count + 3),
        [],
        lower_order,
        *gathered_next,
        w_down_near,
        partial,
        flops=2 * all_rows * model_cols * counts[1],
    )
    received = [over_head(other, at + 1) for at, other in enumerate(others)]
    (final,) = call(
        final_kernel,
        [((share_rows, model_cols), BF16)],
        ["vmem"] * (head_count + 1),
        [],
        residual,
        lowered,
        *received,
    )
    return final


def solution(mesh):
    placed = (
        P(("groups", "branch"), None),
        P(),
        P("branch", "head"),
        P("head"),
        P("branch", "head"),
        P("head"),
        P("branch", "head"),
        P("head"),
        P(("groups", "branch"), None, "head"),
        P(("groups", "branch"), None, "head"),
        P(("groups", "branch")),
        P(("groups", "branch"), None),
        P(("groups", "branch")),
        P("head", "branch"),
        P(),
        P("branch", "head"),
        P("branch", "head"),
        P("head", "branch"),
    )
    return jax.shard_map(
        local,
        mesh=mesh,
        in_specs=placed,
        out_specs=P(("groups", "head"), "branch"),
        check_vma=False,
    )
```

```python
import functools
import math

import jax
import jax.numpy as jnp
import numpy as np
from jax import lax
from jax.experimental import pallas as pl
from jax.experimental.pallas import tpu as pltpu
from jax.sharding import PartitionSpec as P

D = 8192
HD = 128
PAGE = 128
MAXP = 32
POOL = 64
P_DEV = 4
CAP = 8
EXT = 128
CORES = 2

EPS = 1e-06
THETA = 1000000.0
FAR = -1e30
MIB = 1024 * 1024
SPARE = 10 * MIB
SEND_LIMIT = 63 * MIB

F32 = jnp.float32
BF16 = jnp.bfloat16


def hadamard(order_size):
    index = np.arange(order_size)
    common = index[:, None] & index[None, :]
    parity = np.zeros((order_size, order_size), np.int64)
    for bit_level in range(order_size.bit_length() - 1):
        parity = parity ^ (common >> bit_level & 1)
    return ((1 - 2 * parity).astype(np.float32) / np.float32(math.sqrt(order_size))).astype(
        np.float32
    )


SPACES = {"vmem": pltpu.VMEM, "hbm": pltpu.HBM, "any": pl.ANY, "smem": pltpu.SMEM}


def call(kernel, outs, in_spaces, scratch, *args, limit=SPARE, flops=0, moved=0, near=False):
    return pl.pallas_call(
        kernel,
        out_shape=[
            pltpu.VMEM(shape, kind) if near else jax.ShapeDtypeStruct(shape, kind)
            for shape, kind in outs
        ],
        in_specs=[pl.BlockSpec(memory_space=SPACES[space]) for space in in_spaces],
        out_specs=[pl.BlockSpec(memory_space=pltpu.VMEM) for _ in outs],
        scratch_shapes=scratch,
        compiler_params=pltpu.CompilerParams(vmem_limit_bytes=limit),
        cost_estimate=pl.CostEstimate(flops=flops, bytes_accessed=moved, transcendentals=0),
    )(*args)


def fetch_kernel(count, *refs):
    sources, targets, sems = refs[:count], refs[-1 - count : -1], refs[-1]
    copies = [
        pltpu.make_async_copy(source, target, sems.at[at])
        for at, (source, target) in enumerate(zip(sources, targets))
    ]
    for copy in copies:
        copy.start()
    for copy in copies:
        copy.wait()


def fetch(arrays, after, limit=2 * MIB):
    size = sum(array.size * array.dtype.itemsize for array in arrays)
    return pl.pallas_call(
        functools.partial(fetch_kernel, len(arrays)),
        out_shape=[pltpu.VMEM(array.shape, array.dtype) for array in arrays],
        in_specs=[pl.BlockSpec(memory_space=pltpu.HBM)] * len(arrays)
        + [pl.BlockSpec(memory_space=pl.ANY)],
        out_specs=[pl.BlockSpec(memory_space=pltpu.VMEM)] * len(arrays),
        scratch_shapes=[pltpu.SemaphoreType.DMA((len(arrays),))],
        compiler_params=pltpu.CompilerParams(vmem_limit_bytes=limit),
        cost_estimate=pl.CostEstimate(flops=0, bytes_accessed=2 * size, transcendentals=0),
    )(*arrays, after)


def block_width(columns, most):
    best = 128
    for width in range(128, most + 1, 128):
        if columns % width == 0:
            best = width
    return best


class Place:
    def __init__(self, spot, chips, head_count):
        self.chips = chips
        self.head_count = head_count
        self.branch, self.head = spot[0], spot[1]
        self.chip, self.core = self.branch // CORES, self.branch % CORES
        self.steps = [(chip, core) for core in range(CORES) for chip in range(chips)]

    def targets(self):
        return [
            (self.chip + chip) % self.chips * CORES + (self.core + core) % CORES
            for chip, core in self.steps
        ]

    def sources(self):
        return [
            (self.chip + self.chips - chip) % self.chips * CORES + (self.core + core) % CORES
            for chip, core in self.steps
        ]

    def to_heads(self):
        return [(self.head + step) % self.head_count for step in range(self.head_count)]

    def from_heads(self):
        return [
            (self.head + self.head_count - step) % self.head_count
            for step in range(self.head_count)
        ]


def column(devices, length):
    iota = lax.broadcasted_iota(jnp.int32, (length, 1), 0)
    return jnp.concatenate([iota + device * length for device in devices], 0).astype(F32)


def to_row(values):
    size = values.shape[0]
    row_at = lax.broadcasted_iota(jnp.int32, (size, size), 0)
    col_at = lax.broadcasted_iota(jnp.int32, (size, size), 1)
    return jnp.sum(jnp.where(row_at == col_at, values, 0.0), 0, keepdims=True)


def onehot(rows, columns):
    return (rows == to_row(columns)).astype(BF16)


def split_lanes(total):
    rows = total.shape[0]
    high = total.astype(BF16).astype(F32)
    rest = total - high
    middle = rest.astype(BF16).astype(F32)
    low = rest - middle
    lane = lax.broadcasted_iota(jnp.int32, (rows, EXT), 1)
    zero = jnp.zeros((rows, EXT), F32)
    return jnp.where(
        lane == 0, high, jnp.where(lane == 1, middle, jnp.where(lane == 2, low, zero))
    ).astype(BF16)


def split_terms(values, axis):
    high = values.astype(BF16)
    rest = values - high.astype(F32)
    middle = rest.astype(BF16)
    low = (rest - middle.astype(F32)).astype(BF16)
    return jnp.concatenate([high, middle, low], axis)


def dot32(left, right):
    return jnp.dot(left, right, preferred_element_type=F32)


def send_kernel(chips, hidden, parents, *refs):
    blocks, (begun, listed, sems) = refs[:-3], refs[-3:]
    begun[...] = jnp.zeros_like(begun)
    place = Place((lax.axis_index("branch"), 0), chips, 1)
    length, width = hidden.shape[0], blocks[0].shape[1] - EXT
    copies = [pltpu.make_async_copy(parents, listed, sems.at[0])]
    for at, (ref, device) in enumerate(zip(blocks, place.targets())):
        source = hidden.at[:, pl.ds(pl.multiple_of(device * width, width), width)]
        copies.append(pltpu.make_async_copy(source, ref.at[:, :width], sems.at[at + 1]))
    for copy in copies:
        copy.start()
    copies[0].wait()
    row_at = lax.broadcasted_iota(jnp.int32, (length, length), 0)
    col_at = lax.broadcasted_iota(jnp.int32, (length, length), 1)
    turned = jnp.sum(jnp.where(row_at == col_at, listed[...].astype(F32), 0.0), 1, keepdims=True)
    mark = jnp.broadcast_to(turned, (length, EXT)).astype(BF16)
    for ref in blocks:
        ref[:, width:] = mark
    for copy in copies[1:]:
        copy.wait()


def qkv_kernel(slots, chips, head_count, width, *refs):
    spot = refs[0]
    blocks_n = chips * CORES
    blocks = refs[1 : 1 + blocks_n]
    gain, wq, wk, wv, keep, send, share, codes = refs[1 + blocks_n :]
    place = Place(spot, chips, head_count)
    model_cols = gain.shape[1]
    length = blocks[0].shape[0]
    rows = jnp.concatenate([ref[:, :model_cols] for ref in blocks], 0)
    parent = jnp.concatenate([ref[:, model_cols:] for ref in blocks], 0)[:, :1].astype(F32)
    dest = jnp.floor(parent * (1.0 / P_DEV))
    order = column(place.sources(), length)
    order_row = to_row(order)
    same = (dest == to_row(dest)) & (order_row < order)
    code = dest * slots + jnp.sum(same.astype(F32), 1, keepdims=True)
    lane = lax.broadcasted_iota(jnp.int32, codes.shape, 1)
    codes[...] = jnp.where(lane == 0, code, parent)
    placing = onehot(column(place.targets(), slots), code)
    own = column([place.head], share.shape[0])
    share[...] = dot32((own == order_row).astype(BF16), rows).astype(BF16)
    placed = dot32(placing, rows)
    squares = jnp.sum(placed * placed, 1, keepdims=True)
    scaled = (placed * gain[...]).astype(BF16)
    half = keep.shape[0]
    total_cols = keep.shape[1] - EXT
    keep[:, total_cols:] = jnp.broadcast_to(squares[:half], (half, EXT))
    send[:, total_cols:] = jnp.broadcast_to(squares[half:], (half, EXT))
    at = 0
    for weight in (wq, wk, wv):
        wide = block_width(weight.shape[1], width)
        for step in range(weight.shape[1] // wide):
            product = dot32(scaled, weight[:, step * wide : (step + 1) * wide])
            keep[:, at : at + wide] = product[:half]
            send[:, at : at + wide] = product[half:]
            at += wide


def chip_sum_kernel(slots, keep, got, mine, *others):
    mine[...] = keep[:slots] + got[:slots]
    for at, ref in enumerate(others):
        low, high = (at + 1) * slots, (at + 2) * slots
        total = keep[low:high] + got[low:high]
        ref[:, :-EXT] = total[:, :-EXT].astype(BF16)
        ref[:, -EXT:] = split_lanes(total[:, -EXT:][:, :1])


def marks_kernel(
    slots,
    local_rows,
    chips,
    head_count,
    spot,
    path_pages,
    page_table,
    codes,
    waves,
    bq,
    bk,
    bv,
    _,
    wave_out,
    slot_out,
    page_out,
    bias_out,
    mixer_order,
    gate_order,
    lower_order,
):
    place = Place(spot, chips, head_count)
    share_rows = chips * CORES * local_rows // head_count
    code, parent = codes[:, :1], codes[:, 1:2]
    lane = lax.broadcasted_iota(jnp.int32, (1, EXT), 1).astype(F32)
    parent_at = (parent - jnp.floor(parent * (1.0 / P_DEV)) * P_DEV == lane).astype(BF16)
    slot_mark = dot32(onehot(column([spot[0]], slots), code), parent_at)
    wave = jnp.zeros((slots, 2 * HD), F32)
    page_at = lax.broadcasted_iota(jnp.int32, (POOL, MAXP), 0)
    turn_at = lax.broadcasted_iota(jnp.int32, (POOL, MAXP), 1)
    page_mark = jnp.zeros((POOL, EXT), F32)
    for local_parent in range(P_DEV):
        wave = wave + slot_mark[:, local_parent : local_parent + 1] * waves[
            local_parent : local_parent + 1, :
        ]
        live = (page_table[local_parent : local_parent + 1, :] == page_at) & (
            turn_at < path_pages[local_parent]
        )
        owned = jnp.max(live.astype(F32), 1, keepdims=True)
        page_mark = jnp.where(lane == local_parent, (1.0 - owned) * FAR, page_mark)
    wave_out[...] = wave
    slot_out[...] = slot_mark.astype(BF16)
    page_out[...] = page_mark
    bias_out[...] = jnp.concatenate([ref[...].astype(F32) for ref in (bq, bk, bv)], 1)
    child_at = column(place.sources(), local_rows)
    lower = onehot(column(place.to_heads(), share_rows), child_at)
    lower_order[...] = lower
    slot_rows = onehot(code, column(place.sources(), slots))
    mixer_order[...] = dot32(lower, slot_rows).astype(BF16)
    gate_order[...] = onehot(
        column(place.targets(), local_rows), column(place.from_heads(), share_rows)
    )


def attend_kernel(kv_local, group_size, chunk_pages, unroll, received_n, *refs):
    mine = refs[0]
    received = refs[1 : 1 + received_n]
    bias, wave, slot_mark, page_marks, turn, kbuf, vbuf = refs[1 + received_n : 8 + received_n]
    out, scores, mixed = refs[8 + received_n :]
    slots = mine.shape[0]
    squares = mine[:, -EXT:][:, :1]
    total = mine[:, :-EXT]
    for ref in received:
        total = total + ref[:, :-EXT].astype(F32)
        squares = squares + jnp.sum(ref[:, -EXT:].astype(F32), 1, keepdims=True)
    packed = (total * lax.rsqrt(squares * (1.0 / D) + EPS) + bias[...]).astype(BF16).astype(F32)
    heads = kv_local * group_size
    rotation = turn[...]
    def stacked(first, count):
        return jnp.concatenate(
            [packed[:, (first + at) * HD : (first + at + 1) * HD] for at in range(count)], 0
        )

    def rope(vectors, count):
        cos = jnp.concatenate([wave[:, :HD]] * count, 0)
        sin = jnp.concatenate([wave[:, HD:]] * count, 0)
        return vectors * cos + pltpu.roll(vectors, HD // 2, 1) * sin

    queries = rope(stacked(0, heads), heads)
    new_keys = rope(stacked(heads, kv_local), kv_local)
    signs = jnp.where(rotation > 0.0, 1.0, -1.0).astype(BF16)
    even = 1.0 / math.sqrt(HD)
    turned = (
        dot32(split_terms(queries, 1), jnp.concatenate([signs] * 3, 0)) * even
    ).astype(BF16)
    scale = 1.0 / math.sqrt(HD)
    rate = scale * math.log2(math.e)
    rows = group_size * slots
    chunk = chunk_pages * PAGE
    chunks = POOL // chunk_pages
    marks = jnp.concatenate([slot_mark[...]] * group_size, 0)
    for kv_at in range(kv_local):
        query_now = queries[kv_at * rows : (kv_at + 1) * rows]
        left = jnp.concatenate([turned[kv_at * rows : (kv_at + 1) * rows], marks], 1)
        key_now = jnp.concatenate([new_keys[kv_at * slots : (kv_at + 1) * slots]] * group_size, 0)
        own_score = jnp.sum(query_now * key_now, 1, keepdims=True)
        own_row = jnp.broadcast_to(own_score, (rows, HD)).T[:1]
        span = slice(kv_at * HD, (kv_at + 1) * HD)

        def first_pass(at, best):
            pages = pl.ds(pl.multiple_of(at * chunk_pages, chunk_pages), chunk_pages)
            page_keys = kbuf[pages, :, span].reshape(chunk, HD)
            mark = jnp.broadcast_to(
                page_marks[pages, :][:, None, :], (chunk_pages, PAGE, EXT)
            ).reshape(chunk, EXT)
            now = lax.dot_general(
                jnp.concatenate([page_keys, mark.astype(BF16)], 1),
                left,
                (((1,), (1,)), ((), ())),
                preferred_element_type=F32,
            )
            scores[at] = now
            return jnp.maximum(best, jnp.max(now.reshape(chunk // 8, 8, rows), 0))

        best = lax.fori_loop(
            0, chunks, first_pass, jnp.full((8, rows), -jnp.inf, F32), unroll=unroll
        )
        top = jnp.maximum(jnp.max(best, 0, keepdims=True), own_row)
        top_rate = top * rate
        mixed[...] = jnp.zeros_like(mixed)

        def second_pass(at, sums):
            pages = pl.ds(pl.multiple_of(at * chunk_pages, chunk_pages), chunk_pages)
            weights = jnp.exp2(scores[at] * rate - top_rate)
            page_values = vbuf[pages, :, span].reshape(chunk, HD)
            mixed[...] += lax.dot_general(
                page_values,
                weights.astype(BF16),
                (((0,), (0,)), ((), ())),
                preferred_element_type=F32,
            )
            return sums + jnp.sum(weights.reshape(chunk // 8, 8, rows), 0)

        sums = lax.fori_loop(0, chunks, second_pass, jnp.zeros((8, rows), F32), unroll=unroll)
        own = jnp.exp2(own_row * rate - top_rate)
        whole = jnp.sum(sums, 0, keepdims=True) + own
        unturned = (
            dot32(jnp.concatenate([signs] * 3, 1), split_terms(mixed[...], 0)) * even
        )
        value_at = (heads + kv_local + kv_at) * HD
        value_now = jnp.concatenate([packed[:, value_at : value_at + HD]] * group_size, 0)
        result = ((unturned + own * value_now.T) / whole).T.astype(BF16)
        for head in range(group_size):
            at = (kv_at * group_size + head) * HD
            out[:, at : at + HD] = result[head * slots : (head + 1) * slots]


def spread_rows(rows, order, weight, width, mine, others):
    ordered = dot32(order, rows).astype(BF16)
    share = mine.shape[0]
    for step in range(weight.shape[1] // width):
        span = slice(step * width, (step + 1) * width)
        product = dot32(ordered, weight[:, span])
        mine[:, span] = product[:share]
        for at, ref in enumerate(others):
            ref[:, span] = product[(at + 1) * share : (at + 2) * share].astype(BF16)


def mixer_kernel(blocks_n, width, order, *refs):
    blocks = refs[:blocks_n]
    weight, mine = refs[blocks_n : 2 + blocks_n]
    rows = jnp.concatenate([ref[...] for ref in blocks], 0)
    spread_rows(rows, order[...], weight, width, mine, refs[2 + blocks_n :])


def lower_kernel(first, last, blocks_n, share_rows, width, *refs):
    order = refs[0]
    blocks = refs[1 : 1 + blocks_n]
    weight = refs[1 + blocks_n]
    before = None if first == 0 else refs[2 + blocks_n]
    outs = refs[(2 if first == 0 else 3) + blocks_n :]
    rows = jnp.concatenate([ref[...] for ref in blocks], 0)
    ordered = dot32(order[...], rows).astype(BF16)
    deep = rows.shape[1]
    for step in range(weight.shape[1] // width):
        span = slice(step * width, (step + 1) * width)
        product = dot32(ordered, weight[first : first + deep, span])
        if before is not None:
            product = product + before[:, span]
        if not last:
            outs[0][:, span] = product
            continue
        outs[0][:, span] = product[:share_rows]
        for at, ref in enumerate(outs[1:]):
            ref[:, span] = product[(at + 1) * share_rows : (at + 2) * share_rows].astype(BF16)


def residual_kernel(share, mine, gain, *refs):
    received = refs[:-2]
    residual, scaled = refs[-2:]
    total = mine[...]
    for ref in received:
        total = total + ref[...].astype(F32)
    total = share[...].astype(F32) + total
    residual[...] = total
    scaled[:, :-EXT] = (total * gain[...]).astype(BF16)
    scaled[:, -EXT:] = split_lanes(jnp.sum(total * total, 1, keepdims=True))


def gate_columns(ordered, weights, first, count, width, keep, send):
    half = keep.shape[0]
    scaled = ordered[:, :-EXT]
    at = 0
    for weight in weights:
        for step in range(count // width):
            low = first + step * width
            product = dot32(scaled, weight[:, low : low + width])
            keep[:, at : at + width] = product[:half]
            send[:, at : at + width] = product[half:].astype(BF16)
            at += width


def first_gate_kernel(head_count, count, width, *refs):
    order = refs[0]
    blocks = refs[1 : 1 + head_count]
    w_gate, w_up, keep, send, rest = refs[1 + head_count :]
    rows = jnp.concatenate([ref[...] for ref in blocks], 0)
    ordered = dot32(order[...], rows).astype(BF16)
    rest[...] = ordered
    half = keep.shape[0]
    keep[:, -EXT:] = ordered[:half, -EXT:].astype(F32)
    send[:, -EXT:] = ordered[half:, -EXT:]
    gate_columns(ordered, (w_gate, w_up), 0, count, width, keep, send)


def next_gate_kernel(first, count, width, ordered, w_gate, w_up, keep, send):
    gate_columns(ordered[...], (w_gate, w_up), first, count, width, keep, send)


def chip_gate_kernel(local_rows, columns, keep, got, mine, *others):
    mine[...] = keep[:local_rows] + got[:local_rows].astype(F32)
    for at, ref in enumerate(others):
        low, high = (at + 1) * local_rows, (at + 2) * local_rows
        total = keep[low:high] + got[low:high].astype(F32)
        ref[:, :columns] = total[:, :columns].astype(BF16)
        if total.shape[1] > columns:
            ref[:, columns:] = split_lanes(jnp.sum(total[:, columns:], 1, keepdims=True))


def gated(mine, received, columns, scale):
    gate = mine[:, :columns]
    up = mine[:, columns : 2 * columns]
    for ref in received:
        gate = gate + ref[:, :columns].astype(F32)
        up = up + ref[:, columns : 2 * columns].astype(F32)
    gate = gate * scale
    up = up * scale
    return (gate / (1.0 + jnp.exp(-gate)) * up).astype(BF16)


def first_activate_kernel(mine, *refs):
    received, _, out, scale_out = refs[:-3], refs[-3], refs[-2], refs[-1]
    squares = jnp.sum(mine[:, -EXT:], 1, keepdims=True)
    for ref in received:
        squares = squares + jnp.sum(ref[:, -EXT:].astype(F32), 1, keepdims=True)
    scale = lax.rsqrt(squares * (1.0 / D) + EPS)
    scale_out[...] = jnp.broadcast_to(scale, scale_out.shape)
    out[...] = gated(mine, received, out.shape[1], scale)


def next_activate_kernel(scale, mine, *refs):
    out = refs[-1]
    out[...] = gated(mine, refs[:-1], out.shape[1], scale[:, :1])


def final_kernel(residual, mine, *refs):
    received, out = refs[:-1], refs[-1]
    total = mine[...]
    for ref in received:
        total = total + ref[...].astype(F32)
    out[...] = (residual[...] + total).astype(BF16)


def local(
    hidden_in,
    input_gain,
    w_query,
    b_query,
    w_key,
    b_key,
    w_value,
    b_value,
    key_pages,
    value_pages,
    path_pages,
    page_table,
    parent_index,
    w_out,
    post_gain,
    w_gate,
    w_up,
    w_down,
):
    branch_count = lax.axis_size("branch")
    head_count = lax.axis_size("head")
    branch_pos = lax.axis_index("branch")
    head_pos = lax.axis_index("head")
    chips = branch_count // CORES
    local_rows = hidden_in.shape[0]
    all_rows = local_rows * branch_count
    share_rows = all_rows // head_count
    model_cols = w_query.shape[0]
    query_cols = w_query.shape[1]
    kv_cols = w_key.shape[1]
    kv_local = kv_cols // HD
    heads_local = query_cols // HD
    group_size = heads_local // kv_local
    slots = branch_count * CAP
    ff_local = w_gate.shape[1]
    packed_cols = query_cols + 2 * kv_cols
    spot = jnp.stack([branch_pos, head_pos]).astype(jnp.int32)
    steps = [(chip, core) for core in range(CORES) for chip in range(chips)]

    def over_branch(array, chip_step, core_step):
        pairs = []
        for source in range(branch_count):
            chip, core = source // CORES, source % CORES
            to = (chip + chip_step) % chips * CORES + (core + core_step) % CORES
            pairs.append((source, to))
        return lax.ppermute(array, "branch", pairs)

    def over_head(array, step):
        pairs = [(source, (source + step) % head_count) for source in range(head_count)]
        return lax.ppermute(array, "head", pairs)

    def gain_slice(gain):
        return lax.dynamic_slice_in_dim(gain, branch_pos * model_cols, model_cols, 0).astype(F32)[
            None
        ]

    *outgoing, begun = call(
        functools.partial(send_kernel, chips),
        [((local_rows, model_cols + EXT), BF16)] * branch_count + [((8, EXT), F32)],
        ["hbm", "hbm"],
        [pltpu.VMEM((1, local_rows), jnp.int32), pltpu.SemaphoreType.DMA((branch_count + 1,))],
        hidden_in,
        parent_index[None],
        limit=SEND_LIMIT,
        near=True,
    )
    hidden_blocks = [outgoing[0]]
    for block, (chip, core) in zip(outgoing[1:], steps[1:]):
        hidden_blocks.append(over_branch(block, chip, core))
    wq, wk, wv = fetch([w_query, w_key, w_value], begun, 44 * MIB)
    keep, send, share, codes = call(
        functools.partial(qkv_kernel, slots, chips, head_count, 1024),
        [
            ((chips * slots, packed_cols + EXT), F32),
            ((chips * slots, packed_cols + EXT), F32),
            ((share_rows, model_cols), BF16),
            ((all_rows, EXT), F32),
        ],
        ["smem"] + ["vmem"] * (branch_count + 4),
        [],
        spot,
        *hidden_blocks,
        gain_slice(input_gain),
        wq,
        wk,
        wv,
        flops=2 * all_rows * model_cols * packed_cols,
    )
    got = over_branch(send, 0, 1)
    mine, *others = call(
        functools.partial(chip_sum_kernel, slots),
        [((slots, packed_cols + EXT), F32)]
        + [((slots, packed_cols + EXT), BF16)] * (chips - 1),
        ["vmem"] * 2,
        [],
        keep,
        got,
    )
    received = [over_branch(other, at + 1, 0) for at, other in enumerate(others)]
    keys, values = fetch([key_pages, value_pages], others[0])

    freqs = THETA ** (-(jnp.arange(HD // 2, dtype=F32) * 2.0 / HD))
    angle = (path_pages.astype(F32) * PAGE)[:, None] * freqs
    cosine, sine = jnp.cos(angle), jnp.sin(angle)
    waves = jnp.concatenate([cosine, cosine, -sine, sine], 1)
    order_out = ((all_rows, all_rows), BF16)
    wave, slot_mark, page_mark, biases, mixer_order, gate_order, lower_order = call(
        functools.partial(marks_kernel, slots, local_rows, chips, head_count),
        [
            ((slots, 2 * HD), F32),
            ((slots, EXT), BF16),
            ((POOL, EXT), F32),
            ((1, packed_cols), F32),
            ((all_rows, slots * branch_count), BF16),
            order_out,
            order_out,
        ],
        ["smem"] * 2 + ["vmem"] * 6 + ["any"],
        [],
        spot,
        path_pages,
        page_table,
        codes,
        waves,
        b_query[None],
        b_key[None],
        b_value[None],
        others[0],
        moved=MIB,
    )
    rows = group_size * slots
    chunk_pages, unroll = (16, 2) if rows <= 512 else (4, 1)
    score_bytes = 4 * rows * POOL * PAGE
    (attention,) = call(
        functools.partial(attend_kernel, kv_local, group_size, chunk_pages, unroll, chips - 1),
        [((slots, query_cols), BF16)],
        ["vmem"] * (chips + 7),
        [
            pltpu.VMEM((POOL // chunk_pages, chunk_pages * PAGE, rows), F32),
            pltpu.VMEM((HD, rows), F32),
        ],
        mine,
        *received,
        biases,
        wave,
        slot_mark,
        page_mark,
        jnp.asarray(hadamard(HD)),
        keys,
        values,
        limit=score_bytes + SPARE + SPARE // 2,
        flops=4 * kv_cols * rows * POOL * PAGE,
    )

    def gather_branch(array):
        near = [array] + [over_branch(array, chip, 0) for chip in range(1, chips)]
        return near + [over_branch(block, 0, 1) for block in near]

    gathered = gather_branch(attention)
    (w_out_near,) = fetch([w_out], attention)
    out_width = block_width(model_cols, 2048)
    mixer, *others = call(
        functools.partial(mixer_kernel, branch_count, out_width),
        [((share_rows, model_cols), F32)] + [((share_rows, model_cols), BF16)] * (head_count - 1),
        ["vmem"] * (branch_count + 2),
        [],
        mixer_order,
        *gathered,
        w_out_near,
        flops=2 * all_rows * w_out.size,
    )
    received = [over_head(other, at + 1) for at, other in enumerate(others)]
    (w_gate_near,) = fetch([w_gate], mixer)
    residual, scaled = call(
        residual_kernel,
        [((share_rows, model_cols), F32), ((share_rows, model_cols + EXT), BF16)],
        ["vmem"] * (head_count + 2),
        [],
        share,
        mixer,
        gain_slice(post_gain),
        *received,
    )
    scaled_blocks = [scaled] + [over_head(scaled, step) for step in range(1, head_count)]
    (w_up_near,) = fetch([w_up], scaled)
    tiles = ff_local // 128
    cuts = [0, (tiles + 1) // 2 * 128, ff_local]
    counts = [high - low for low, high in zip(cuts, cuts[1:])]

    def gate_outs(extra):
        return [((chips * local_rows, extra), F32), ((chips * local_rows, extra), BF16)]

    keep, send, ordered = call(
        functools.partial(
            first_gate_kernel,
            head_count,
            counts[0],
            block_width(counts[0], 1920),
        ),
        gate_outs(2 * counts[0] + EXT) + [((all_rows, model_cols + EXT), BF16)],
        ["vmem"] * (head_count + 3),
        [],
        gate_order,
        *scaled_blocks,
        w_gate_near,
        w_up_near,
        flops=4 * all_rows * model_cols * counts[0],
    )
    parts = [(keep, over_branch(send, 0, 1))]
    keep, send = call(
        functools.partial(next_gate_kernel, cuts[1], counts[1], block_width(counts[1], 1920)),
        gate_outs(2 * counts[1]),
        ["vmem"] * 3,
        [],
        ordered,
        w_gate_near,
        w_up_near,
        flops=4 * all_rows * model_cols * counts[1],
    )
    parts.append((keep, over_branch(send, 0, 1)))
    sums = []
    for (keep, got), count in zip(parts, counts):
        wide = keep.shape[1]
        mine, *others = call(
            functools.partial(chip_gate_kernel, local_rows, 2 * count),
            [((local_rows, wide), F32)] + [((local_rows, wide), BF16)] * (chips - 1),
            ["vmem"] * 2,
            [],
            keep,
            got,
        )
        sums.append((mine, [over_branch(other, at + 1, 0) for at, other in enumerate(others)], others))
    (w_down_near,) = fetch([w_down], sums[1][2][0], 32 * MIB)
    activated, scale = call(
        first_activate_kernel,
        [((local_rows, counts[0]), BF16), ((local_rows, EXT), F32)],
        ["vmem"] * chips + ["any"],
        [],
        sums[0][0],
        *sums[0][1],
        w_down_near,
    )
    gathered = gather_branch(activated)
    (activated,) = call(
        next_activate_kernel,
        [((local_rows, counts[1]), BF16)],
        ["vmem"] * (chips + 1),
        [],
        scale,
        sums[1][0],
        *sums[1][1],
    )
    gathered_next = gather_branch(activated)
    (partial,) = call(
        functools.partial(lower_kernel, 0, False, branch_count, share_rows, out_width),
        [((all_rows, model_cols), F32)],
        ["vmem"] * (branch_count + 2),
        [],
        lower_order,
        *gathered,
        w_down_near,
        flops=2 * all_rows * model_cols * counts[0],
    )
    lowered, *others = call(
        functools.partial(lower_kernel, cuts[1], True, branch_count, share_rows, out_width),
        [((share_rows, model_cols), F32)] + [((share_rows, model_cols), BF16)] * (head_count - 1),
        ["vmem"] * (branch_count + 3),
        [],
        lower_order,
        *gathered_next,
        w_down_near,
        partial,
        flops=2 * all_rows * model_cols * counts[1],
    )
    received = [over_head(other, at + 1) for at, other in enumerate(others)]
    (final,) = call(
        final_kernel,
        [((share_rows, model_cols), BF16)],
        ["vmem"] * (head_count + 1),
        [],
        residual,
        lowered,
        *received,
    )
    return final


def solution(mesh):
    placed = (
        P(("groups", "branch"), None),
        P(),
        P("branch", "head"),
        P("head"),
        P("branch", "head"),
        P("head"),
        P("branch", "head"),
        P("head"),
        P(("groups", "branch"), None, "head"),
        P(("groups", "branch"), None, "head"),
        P(("groups", "branch")),
        P(("groups", "branch"), None),
        P(("groups", "branch")),
        P("head", "branch"),
        P(),
        P("branch", "head"),
        P("branch", "head"),
        P("head", "branch"),
    )
    return jax.shard_map(
        local,
        mesh=mesh,
        in_specs=placed,
        out_specs=P(("groups", "head"), "branch"),
        check_vma=False,
    )
```
